512 devices in a mesh: dom: 64 (over z_hi, y, x, core), feat: 8 (over z_lo).
Axes of the slice: x: 4, y: 4, z: 16 (z_hi: 2, z_lo: 8; z = z_hi * 8 + z_lo), core: 2. Of those that a mesh axis runs over, the one named last changes fastest.
Arguments:
- features: bfloat16 [256, 851968], P('feat', 'dom'), may hold values from -6 to 6
- block_row: int32 [64, 64], P('dom'), may hold values from 0 to 103, as said below
- block_col: int32 [64, 64], P('dom'), may hold values from 0 to 119, as said below
- block_count: int32 [64], P('dom'), may hold values from 2 to 64, as said below
- block_values: bfloat16 [4096, 128, 128], P('dom'), may hold values from -0.5 to 0.5
- w_self: bfloat16 [256, 256], replicated, may hold values from -0.375 to 0.375
- w_neigh: bfloat16 [256, 256], replicated, may hold values from -0.375 to 0.375
- cotangent: bfloat16 [256, 851968], P(None, ('dom', 'feat')), may hold values from -6 to 6
Outputs:
- feature_grad: bfloat16 [256, 851968], P('feat', 'dom')
- self_grad: bfloat16 [256, 256], replicated
- neigh_grad: bfloat16 [256, 256], replicated
The draws below stay inside these ranges and needn't reach their ends.
Inputs may be any that keep to these rules, and one draw needn't show every extreme that they name: `block_row`: in every partition slot 0 lies in block row 0 and slot 1 in block row 103. block_col differs from block_row + 8 by at most 8; in every partition slot 0 has the value 0 and slot 1 the value 104 + 2 * 8 - 1. `block_count`: some partition uses all 64 slots in every draw.
All inputs are finite; a program needn't handle non-finite values.
Results may differ from the reference program's by a relative error of at most 0.0061.
Values may be sent and summed in bfloat16 or wider, within the bound.
No kernel may reach another device: no remote copies, remote signals or barrier semaphores. Data moves between devices by JAX's collectives and lax.ppermute only.
A program may use at most 64 MiB of HBM per device.

```python
import math
import jax
import jax.numpy as jnp
from jax import lax

D = 256
BLK = 128
REACH = 8
ROW_BLOCKS = 104
BLOCKS = 64
PARTS_SIZE = 64
NODES = 851968


def adjacency_pattern(key):
    first_key, second_key = jax.random.split(key)
    block_rows = jax.random.randint(first_key, (PARTS_SIZE, BLOCKS), 0, ROW_BLOCKS, dtype=jnp.int32)
    offsets = jax.random.randint(second_key, (PARTS_SIZE, BLOCKS), -REACH, REACH + 1, dtype=jnp.int32)
    block_cols = block_rows + REACH + offsets
    block_rows = block_rows.at[:, 0].set(0).at[:, 1].set(ROW_BLOCKS - 1)
    block_cols = block_cols.at[:, 0].set(0).at[:, 1].set(ROW_BLOCKS + 2 * REACH - 1)
    return (block_rows, block_cols)


def draw_block_row(key, part):
    block_rows, block_cols = adjacency_pattern(key)
    return block_rows


def draw_block_col(key, part):
    block_rows, block_cols = adjacency_pattern(key)
    return block_cols


def draw_block_count(key, part):
    key = jax.random.fold_in(key, 11)
    first_key, second_key, third_key = jax.random.split(key, 3)
    base = jax.random.randint(first_key, (PARTS_SIZE,), 2, BLOCKS // 2 + 1, dtype=jnp.int32)
    busy = jax.random.randint(second_key, (PARTS_SIZE,), 0, 8, dtype=jnp.int32) == 0
    counts = jnp.where(busy, BLOCKS, base).astype(jnp.int32)
    chosen = jax.random.randint(third_key, (), 0, PARTS_SIZE, dtype=jnp.int32)
    return counts.at[chosen].set(BLOCKS)


def level_of(key, shape, shards, least, largest):
    def one(dim, blocks):
        steps = jax.random.uniform(jax.random.fold_in(jax.random.fold_in(key, 6), dim), (blocks,), jnp.float32, least / len(shards), largest / len(shards))
        return jnp.repeat(jnp.exp(steps), shape[dim] // blocks).reshape((-1,) + (1,) * (len(shape) - dim - 1))

    loudness = one(*shards[0])
    for cut in shards[1:]:
        loudness = loudness * one(*cut)
    return loudness


def scatter_about(rng, extent, scale, limit, cuts=(), kind=jnp.bfloat16):
    gain = level_of(rng, extent, cuts, -0.22, 0.18) if cuts else 1.0
    entries = jax.random.normal(rng, extent, jnp.float32) * scale * gain
    return jnp.minimum(jnp.maximum(entries, -limit), limit).astype(kind)


def setup_inputs(seed: int = 0) -> dict:
    key_of = jax.random.split(jax.random.key(seed), 9)
    features = scatter_about(key_of[0], (D, NODES), 1.0, 6.0, ((0, 8), (1, 64)))
    block_row = draw_block_row(jax.random.fold_in(key_of[8], 71), 0)
    block_col = draw_block_col(jax.random.fold_in(key_of[8], 71), 0)
    block_count = draw_block_count(jax.random.fold_in(key_of[8], 71), 0)
    block_values = scatter_about(key_of[4], (PARTS_SIZE * BLOCKS, BLK, BLK), BLK ** -0.5, 0.5, ((0, 64),))
    w_self = scatter_about(key_of[5], (D, D), D ** -0.5, 0.375)
    w_neigh = scatter_about(key_of[6], (D, D), D ** -0.5, 0.375)
    cotangent = scatter_about(key_of[7], (D, NODES), 1.0, 6.0, ((1, 512),))
    return dict(features=features, block_row=block_row, block_col=block_col, block_count=block_count, block_values=block_values, w_self=w_self, w_neigh=w_neigh, cotangent=cotangent)


def silu_slope(preact):
    sigma = jax.nn.sigmoid(preact)
    return sigma * (1.0 + preact * (1.0 - sigma))

def reference(features, block_row, block_col, block_count, block_values, w_self, w_neigh, cotangent):
    rim = REACH * BLK
    rows_part = ROW_BLOCKS * BLK
    widened_blocks = ROW_BLOCKS + 2 * REACH
    feat_parts = features.reshape(D, PARTS_SIZE, rows_part)
    grad_parts = cotangent.reshape(D, PARTS_SIZE, rows_part)
    value_parts = block_values.reshape(PARTS_SIZE, BLOCKS, BLK, BLK)

    def partition(index):
        local_part = lax.dynamic_index_in_dim(feat_parts, index, 1, keepdims=False)
        before = lax.dynamic_index_in_dim(feat_parts, (index + PARTS_SIZE - 1) % PARTS_SIZE, 1, keepdims=False)
        after = lax.dynamic_index_in_dim(feat_parts, (index + 1) % PARTS_SIZE, 1, keepdims=False)
        widened = jnp.concatenate([before[:, rows_part - rim:], local_part, after[:, :rim]], axis=1)
        block_rows = lax.dynamic_index_in_dim(block_row, index, 0, keepdims=False)
        block_cols = lax.dynamic_index_in_dim(block_col, index, 0, keepdims=False)
        count = lax.dynamic_index_in_dim(block_count, index, 0, keepdims=False)
        values = lax.dynamic_index_in_dim(value_parts, index, 0, keepdims=False).astype(jnp.float32)
        live = (jnp.arange(BLOCKS, dtype=jnp.int32) < count).astype(jnp.float32)
        columns = jnp.take(widened.reshape(D, widened_blocks, BLK), block_cols, axis=1)
        products = jnp.einsum('dkj,kij->dki', columns.astype(jnp.float32), values) * live[None, :, None]
        row_onehot = (jnp.arange(ROW_BLOCKS, dtype=jnp.int32)[:, None] == block_rows[None, :]).astype(jnp.float32)
        aggregated = jnp.einsum('rk,dki->dri', row_onehot, products, precision=lax.Precision.HIGHEST)
        aggregated = aggregated.reshape(D, rows_part).astype(jnp.bfloat16)
        upstream = lax.dynamic_index_in_dim(grad_parts, index, 1, keepdims=False)
        preact = jnp.dot(w_self.T, local_part, preferred_element_type=jnp.float32)
        preact = preact + jnp.dot(w_neigh.T, aggregated, preferred_element_type=jnp.float32)
        delta = (upstream.astype(jnp.float32) * silu_slope(preact)).astype(jnp.bfloat16)
        self_term = jnp.dot(local_part, delta.T, preferred_element_type=jnp.float32)
        neigh_term = jnp.dot(aggregated, delta.T, preferred_element_type=jnp.float32)
        direct = jnp.dot(w_self, delta, preferred_element_type=jnp.float32).astype(jnp.bfloat16)
        agg_grad = jnp.dot(w_neigh, delta, preferred_element_type=jnp.float32).astype(jnp.bfloat16)
        picked = jnp.take(agg_grad.reshape(D, ROW_BLOCKS, BLK), block_rows, axis=1)
        spread = jnp.einsum('dki,kij->dkj', picked.astype(jnp.float32), values) * live[None, :, None]
        col_onehot = (jnp.arange(widened_blocks, dtype=jnp.int32)[:, None] == block_cols[None, :]).astype(jnp.float32)
        scattered = jnp.einsum('ek,dkj->dej', col_onehot, spread, precision=lax.Precision.HIGHEST)
        scattered = scattered.reshape(D, widened_blocks * BLK)
        middle = direct.astype(jnp.float32) + scattered[:, rim:rim + rows_part]
        return (middle, scattered[:, :rim], scattered[:, rim + rows_part:], self_term, neigh_term)
    middle, lefts, rights, self_terms, neigh_terms = lax.map(partition, jnp.arange(PARTS_SIZE, dtype=jnp.int32))
    from_next = jnp.roll(lefts, -1, axis=0)
    from_prev = jnp.roll(rights, 1, axis=0)
    total = middle + jnp.pad(from_prev, ((0, 0), (0, 0), (0, rows_part - rim)))
    total = total + jnp.pad(from_next, ((0, 0), (0, 0), (rows_part - rim, 0)))
    feature_grad = total.transpose(1, 0, 2).reshape(D, NODES).astype(jnp.bfloat16)
    factor = 1.0 / math.sqrt(NODES)
    self_grad = (lax.optimization_barrier(jnp.sum(self_terms, axis=0)) * factor).astype(jnp.bfloat16)
    neigh_grad = (lax.optimization_barrier(jnp.sum(neigh_terms, axis=0)) * factor).astype(jnp.bfloat16)
    return (feature_grad, self_grad, neigh_grad)
```

```python
import functools
import math

import jax
import jax.numpy as jnp
from jax import lax
from jax.experimental import pallas as pl
from jax.experimental.pallas import tpu as pltpu
from jax.sharding import Mesh, PartitionSpec as P

BLK = 128
REACH = 8
DOM = ("zh", "y", "x", "core")
PLANE = ("y", "x", "core")
LINE = ("zh", "feat")
RING = DOM + ("feat",)


def shifted(shard, axis, by):
    count = lax.axis_size(axis)
    return lax.ppermute(shard, axis, [(i, (i + by) % count) for i in range(count)])


def tiles_of(width, tile):
    return [(at, min(tile, width - at)) for at in range(0, width, tile)]


def local_kernel(
    rows_ref,
    cols_ref,
    count_ref,
    pos_ref,
    own_ref,
    before_ref,
    after_ref,
    values_ref,
    w_in_ref,
    w_out_ref,
    cot_ref,
    middle_ref,
    left_ref,
    right_ref,
    terms_ref,
    wide,
    agg,
    stacked,
    delta,
    agg_grad,
    scat,
    sems,
):
    depth, width = own_ref.shape
    rim = before_ref.shape[1]
    chunk = width // BLK
    copies = [
        pltpu.make_async_copy(before_ref, wide.at[:, pl.ds(0, rim)], sems.at[0]),
        pltpu.make_async_copy(own_ref, wide.at[:, pl.ds(rim, width)], sems.at[1]),
        pltpu.make_async_copy(after_ref, wide.at[:, pl.ds(rim + width, rim)], sems.at[2]),
    ]
    for copy in copies:
        copy.start()
    agg[...] = jnp.zeros_like(agg)
    scat[:, :rim] = jnp.zeros((depth, rim), jnp.float32)
    scat[:, rim + width :] = jnp.zeros((depth, rim), jnp.float32)
    first = pos_ref[0] * chunk
    count = count_ref[0]
    for copy in copies:
        copy.wait()

    def gather_slot(slot, carry):
        row = rows_ref[slot] - first

        @pl.when((row >= 0) & (row < chunk))
        def _():
            col = cols_ref[slot] - first
            source = wide[:, pl.ds(pl.multiple_of(col * BLK, BLK), BLK)]
            into = pl.ds(pl.multiple_of(row * BLK, BLK), BLK)
            agg[:, into] += lax.dot_general(
                source,
                values_ref[slot],
                (((1,), (1,)), ((), ())),
                preferred_element_type=jnp.float32,
            )

        return carry

    lax.fori_loop(0, count, gather_slot, 0)

    for at, size in tiles_of(width, 256):
        part = slice(at, at + size)
        stacked[:depth, part] = wide[:, rim + at : rim + at + size]
        stacked[depth:, part] = agg[:, part].astype(jnp.bfloat16)
        preact = jnp.dot(w_in_ref[...], stacked[:, part], preferred_element_type=jnp.float32)
        sigma = 1.0 / (1.0 + jnp.exp(-preact))
        slope = sigma * (1.0 + preact * (1.0 - sigma))
        delta[:, part] = (cot_ref[:, part].astype(jnp.float32) * slope).astype(jnp.bfloat16)
        both = jnp.dot(w_out_ref[...], delta[:, part], preferred_element_type=jnp.float32)
        both = both.astype(jnp.bfloat16)
        scat[:, rim + at : rim + at + size] = both[:depth].astype(jnp.float32)
        agg_grad[:, part] = both[depth:]

    def scatter_slot(slot, carry):
        row = rows_ref[slot] - first

        @pl.when((row >= 0) & (row < chunk))
        def _():
            col = cols_ref[slot] - first
            source = agg_grad[:, pl.ds(pl.multiple_of(row * BLK, BLK), BLK)]
            into = pl.ds(pl.multiple_of(col * BLK, BLK), BLK)
            scat[:, into] += jnp.dot(
                source, values_ref[slot], preferred_element_type=jnp.float32
            )

        return carry

    lax.fori_loop(0, count, scatter_slot, 0)
    left_ref[...] = scat[:, :rim].astype(jnp.bfloat16)
    right_ref[...] = scat[:, rim + width :].astype(jnp.bfloat16)
    middle_ref[...] = scat[:, rim : rim + width]
    terms_ref[...] = lax.dot_general(
        stacked[...], delta[...], (((1,), (1,)), ((), ())), preferred_element_type=jnp.float32
    )


def local_step(rows, cols, count, pos, own, before, after, values, w_in, w_out, cot):
    depth, width = own.shape
    rim = before.shape[1]
    smem = pl.BlockSpec(memory_space=pltpu.SMEM)
    vmem = pl.BlockSpec(memory_space=pltpu.VMEM)
    anywhere = pl.BlockSpec(memory_space=pl.ANY)
    return pl.pallas_call(
        local_kernel,
        out_shape=(
            jax.ShapeDtypeStruct((depth, width), jnp.float32),
            jax.ShapeDtypeStruct((depth, rim), jnp.bfloat16),
            jax.ShapeDtypeStruct((depth, rim), jnp.bfloat16),
            jax.ShapeDtypeStruct((2 * depth, depth), jnp.float32),
        ),
        in_specs=[smem] * 4 + [anywhere] * 3 + [vmem] * 4,
        out_specs=(vmem,) * 4,
        scratch_shapes=[
            pltpu.VMEM((depth, width + 2 * rim), jnp.bfloat16),
            pltpu.VMEM((depth, width), jnp.float32),
            pltpu.VMEM((2 * depth, width), jnp.bfloat16),
            pltpu.VMEM((depth, width), jnp.bfloat16),
            pltpu.VMEM((depth, width), jnp.bfloat16),
            pltpu.VMEM((depth, width + 2 * rim), jnp.float32),
            pltpu.SemaphoreType.DMA((3,)),
        ],
        compiler_params=pltpu.CompilerParams(vmem_limit_bytes=48 * 1024 * 1024),
        cost_estimate=pl.CostEstimate(
            flops=12 * depth * depth * width, bytes_accessed=8 << 20, transcendentals=depth * width
        ),
    )(rows, cols, count, pos, own, before, after, values, w_in, w_out, cot)


def on_device(
    features, block_row, block_col, block_count, block_values, w_self, w_neigh, cotangent
):
    rows_part = features.shape[1]
    depth, width = cotangent.shape
    rim = REACH * BLK
    own = lax.all_to_all(features, "feat", split_axis=1, concat_axis=0, tiled=True)
    before = shifted(own[:, width - rim :], RING, 1)
    after = shifted(own[:, :rim], RING, -1)
    w_in = jnp.concatenate([w_self.T, w_neigh.T], axis=1)
    w_out = jnp.concatenate([w_self, w_neigh], axis=0)
    pos = lax.axis_index("feat").astype(jnp.int32)[None]
    middle, left, right, terms = local_step(
        block_row[0],
        block_col[0],
        block_count,
        pos,
        own,
        before,
        after,
        block_values,
        w_in,
        w_out,
        cotangent,
    )
    from_next = shifted(left, RING, -1).astype(jnp.float32)
    from_prev = shifted(right, RING, 1).astype(jnp.float32)
    total = middle + jnp.pad(from_prev, ((0, 0), (0, width - rim)))
    total = total + jnp.pad(from_next, ((0, 0), (width - rim, 0)))
    total = total.astype(jnp.bfloat16)
    feature_grad = lax.all_to_all(total, "feat", split_axis=0, concat_axis=1, tiled=True)

    plane, line = lax.axis_size(PLANE), lax.axis_size(LINE)
    share = 2 * depth // plane
    pieces = lax.all_to_all(terms, PLANE, split_axis=0, concat_axis=0, tiled=True)
    partial = pieces.reshape(plane, share, depth).sum(0)
    copies = jnp.broadcast_to(partial[None], (line, share, depth))
    copies = lax.all_to_all(copies, LINE, split_axis=0, concat_axis=0, tiled=True)
    factor = 1.0 / math.sqrt(rows_part * lax.axis_size(DOM))
    grads = (copies.sum(0) * factor).astype(jnp.bfloat16)
    grads = jnp.broadcast_to(grads[None], (plane, share, depth))
    grads = lax.all_to_all(grads, PLANE, split_axis=0, concat_axis=0, tiled=True)
    grads = grads.reshape(2 * depth, depth)
    return (feature_grad, grads[:depth], grads[depth:])


def solution(mesh):
    fine = Mesh(mesh.devices.reshape(2, 4, 4, 2, 8), RING)
    return jax.shard_map(
        on_device,
        mesh=fine,
        in_specs=(
            P("feat", DOM),
            P(DOM, None),
            P(DOM, None),
            P(DOM),
            P(DOM, None, None),
            P(),
            P(),
            P(None, RING),
        ),
        out_specs=(P("feat", DOM), P(), P()),
        check_vma=False,
    )
```

```python
import functools
import math

import jax
import jax.numpy as jnp
from jax import lax
from jax.experimental import pallas as pl
from jax.experimental.pallas import tpu as pltpu
from jax.sharding import Mesh, PartitionSpec as P

BLK = 128
REACH = 8
DOM = ("zh", "y", "x", "core")
PLANE = ("y", "x", "core")
LINE = ("zh", "feat")
RING = DOM + ("feat",)
EARLY = (4, 2, 6, 1)
LATE = (3, 5, 7)


def shifted(shard, axis, by):
    count = lax.axis_size(axis)
    return lax.ppermute(shard, axis, [(i, (i + by) % count) for i in range(count)])


def tiles_of(width, tile):
    return [(at, min(tile, width - at)) for at in range(0, width, tile)]


def local_kernel(
    rows_ref,
    cols_ref,
    count_ref,
    pos_ref,
    own_ref,
    before_ref,
    after_ref,
    values_ref,
    w_in_ref,
    w_out_ref,
    cot_ref,
    middle_ref,
    left_ref,
    right_ref,
    stacked,
    delta,
    wide,
    agg,
    agg_grad,
    scat,
    sems,
):
    depth, width = own_ref.shape
    rim = before_ref.shape[1]
    chunk = width // BLK
    copies = [
        pltpu.make_async_copy(before_ref, wide.at[:, pl.ds(0, rim)], sems.at[0]),
        pltpu.make_async_copy(own_ref, wide.at[:, pl.ds(rim, width)], sems.at[1]),
        pltpu.make_async_copy(after_ref, wide.at[:, pl.ds(rim + width, rim)], sems.at[2]),
    ]
    for copy in copies:
        copy.start()
    agg[...] = jnp.zeros_like(agg)
    scat[:, :rim] = jnp.zeros((depth, rim), jnp.float32)
    scat[:, rim + width :] = jnp.zeros((depth, rim), jnp.float32)
    first = pos_ref[0] * chunk
    count = count_ref[0]
    for copy in copies:
        copy.wait()

    def gather_slot(slot, carry):
        row = rows_ref[slot] - first

        @pl.when((row >= 0) & (row < chunk))
        def _():
            col = cols_ref[slot] - first
            source = wide[:, pl.ds(pl.multiple_of(col * BLK, BLK), BLK)]
            into = pl.ds(pl.multiple_of(row * BLK, BLK), BLK)
            agg[:, into] += lax.dot_general(
                source,
                values_ref[slot],
                (((1,), (1,)), ((), ())),
                preferred_element_type=jnp.float32,
            )

        return carry

    lax.fori_loop(0, count, gather_slot, 0)

    for at, size in tiles_of(width, 256):
        part = slice(at, at + size)
        stacked[:depth, part] = wide[:, rim + at : rim + at + size]
        stacked[depth:, part] = agg[:, part].astype(jnp.bfloat16)
        preact = jnp.dot(w_in_ref[...], stacked[:, part], preferred_element_type=jnp.float32)
        sigma = 1.0 / (1.0 + jnp.exp(-preact))
        slope = sigma * (1.0 + preact * (1.0 - sigma))
        delta[:, part] = (cot_ref[:, part].astype(jnp.float32) * slope).astype(jnp.bfloat16)
        both = jnp.dot(w_out_ref[...], delta[:, part], preferred_element_type=jnp.float32)
        both = both.astype(jnp.bfloat16)
        scat[:, rim + at : rim + at + size] = both[:depth].astype(jnp.float32)
        agg_grad[:, part] = both[depth:]

    def scatter_slot(slot, carry):
        row = rows_ref[slot] - first

        @pl.when((row >= 0) & (row < chunk))
        def _():
            col = cols_ref[slot] - first
            source = agg_grad[:, pl.ds(pl.multiple_of(row * BLK, BLK), BLK)]
            into = pl.ds(pl.multiple_of(col * BLK, BLK), BLK)
            scat[:, into] += jnp.dot(
                source, values_ref[slot], preferred_element_type=jnp.float32
            )

        return carry

    lax.fori_loop(0, count, scatter_slot, 0)
    left_ref[...] = scat[:, :rim].astype(jnp.bfloat16)
    right_ref[...] = scat[:, rim + width :].astype(jnp.bfloat16)
    middle_ref[...] = scat[:, rim : rim + width]


def send_kernel(pos_ref, middle_ref, prev_ref, next_ref, *piece_refs):
    pieces = len(piece_refs)
    height, width = piece_refs[0].shape
    rim = prev_ref.shape[1]
    for step, piece_ref in enumerate(piece_refs):
        dest = lax.rem(pos_ref[0] + step, pieces)
        rows = pl.ds(pl.multiple_of(dest * height, height), height)
        for at, size in ((0, width - rim), (width - rim, 2 * rim - width), (rim, width - rim)):
            part = middle_ref[rows, at : at + size]
            if at < rim:
                part = part + prev_ref[rows, at : at + size].astype(jnp.float32)
            if at >= width - rim:
                here = at - (width - rim)
                part = part + next_ref[rows, here : here + size].astype(jnp.float32)
            piece_ref[:, at : at + size] = part.astype(jnp.bfloat16)


def send_step(pos, middle, prev_part, next_part, pieces):
    depth, width = middle.shape
    vmem = pl.BlockSpec(memory_space=pltpu.VMEM)
    return pl.pallas_call(
        send_kernel,
        out_shape=(jax.ShapeDtypeStruct((depth // pieces, width), jnp.bfloat16),) * pieces,
        in_specs=[pl.BlockSpec(memory_space=pltpu.SMEM)] + [vmem] * 3,
        out_specs=(vmem,) * pieces,
        compiler_params=pltpu.CompilerParams(vmem_limit_bytes=32 * 1024 * 1024),
        cost_estimate=pl.CostEstimate(flops=0, bytes_accessed=4 << 20, transcendentals=0),
    )(pos, middle, prev_part, next_part)


def place_kernel(pos_ref, *refs):
    piece_refs, out_ref, sems = refs[:-2], refs[-2], refs[-1]
    pieces = len(piece_refs)
    width = piece_refs[0].shape[1]
    copies = []
    for step, piece_ref in enumerate(piece_refs):
        source = lax.rem(pos_ref[0] + pieces - step, pieces)
        into = pl.ds(pl.multiple_of(source * width, BLK), width)
        copies.append(pltpu.make_async_copy(piece_ref, out_ref.at[:, into], sems.at[step]))
    for copy in copies:
        copy.start()
    for copy in copies:
        copy.wait()


def place_step(pos, received):
    pieces = len(received)
    height, width = received[0].shape
    anywhere = pl.BlockSpec(memory_space=pl.ANY)
    return pl.pallas_call(
        place_kernel,
        out_shape=jax.ShapeDtypeStruct((height, pieces * width), jnp.bfloat16),
        in_specs=[pl.BlockSpec(memory_space=pltpu.SMEM)] + [anywhere] * pieces,
        out_specs=anywhere,
        scratch_shapes=[pltpu.SemaphoreType.DMA((pieces,))],
        cost_estimate=pl.CostEstimate(flops=0, bytes_accessed=2 << 20, transcendentals=0),
    )(pos, *received)


def local_step(rows, cols, count, pos, own, before, after, values, w_in, w_out, cot):
    depth, width = own.shape
    rim = before.shape[1]
    smem = pl.BlockSpec(memory_space=pltpu.SMEM)
    vmem = pl.BlockSpec(memory_space=pltpu.VMEM)
    anywhere = pl.BlockSpec(memory_space=pl.ANY)
    return pl.pallas_call(
        local_kernel,
        out_shape=(
            jax.ShapeDtypeStruct((depth, width), jnp.float32),
            jax.ShapeDtypeStruct((depth, rim), jnp.bfloat16),
            jax.ShapeDtypeStruct((depth, rim), jnp.bfloat16),
            jax.ShapeDtypeStruct((2 * depth, width), jnp.bfloat16),
            jax.ShapeDtypeStruct((depth, width), jnp.bfloat16),
        ),
        in_specs=[smem] * 4 + [anywhere] * 3 + [vmem] * 4,
        out_specs=(vmem,) * 5,
        scratch_shapes=[
            pltpu.VMEM((depth, width + 2 * rim), jnp.bfloat16),
            pltpu.VMEM((depth, width), jnp.float32),
            pltpu.VMEM((depth, width), jnp.bfloat16),
            pltpu.VMEM((depth, width + 2 * rim), jnp.float32),
            pltpu.SemaphoreType.DMA((3,)),
        ],
        compiler_params=pltpu.CompilerParams(vmem_limit_bytes=48 * 1024 * 1024),
        cost_estimate=pl.CostEstimate(
            flops=12 * depth * depth * width, bytes_accessed=8 << 20, transcendentals=depth * width
        ),
    )(rows, cols, count, pos, own, before, after, values, w_in, w_out, cot)


def on_device(
    features, block_row, block_col, block_count, block_values, w_self, w_neigh, cotangent
):
    rows_part = features.shape[1]
    depth, width = cotangent.shape
    rim = REACH * BLK
    own = lax.all_to_all(features, "feat", split_axis=1, concat_axis=0, tiled=True)
    before = shifted(own[:, width - rim :], RING, 1)
    after = shifted(own[:, :rim], RING, -1)
    w_in = jnp.concatenate([w_self.T, w_neigh.T], axis=1)
    w_out = jnp.concatenate([w_self, w_neigh], axis=0)
    pos = lax.axis_index("feat").astype(jnp.int32)[None]
    middle, left, right, stacked, delta = local_step(
        block_row[0],
        block_col[0],
        block_count,
        pos,
        own,
        before,
        after,
        block_values,
        w_in,
        w_out,
        cotangent,
    )
    from_next = shifted(left, RING, -1)
    from_prev = shifted(right, RING, 1)
    pieces = lax.axis_size("feat")
    to_send = list(send_step(pos, middle, from_prev, from_next, pieces))

    terms = jnp.einsum("in,on->io", stacked, delta, preferred_element_type=jnp.float32)
    plane, line = lax.axis_size(PLANE), lax.axis_size(LINE)
    share = 2 * depth // plane
    parts = lax.all_to_all(terms, PLANE, split_axis=0, concat_axis=0, tiled=True)
    partial = parts.reshape(plane, share, depth).sum(0)
    partial, to_send[0] = lax.optimization_barrier((partial, to_send[0]))
    copies = jnp.broadcast_to(partial[None], (line, share, depth))
    copies = lax.all_to_all(copies, LINE, split_axis=0, concat_axis=0, tiled=True)
    factor = 1.0 / math.sqrt(rows_part * lax.axis_size(DOM))
    grads = (copies.sum(0) * factor).astype(jnp.bfloat16)
    received = {0: to_send[0]}
    for step in EARLY:
        received[step] = shifted(to_send[step], "feat", step)
    steps = EARLY + LATE
    held = [received[step] for step in EARLY] + [to_send[step] for step in LATE]
    grads, *held = lax.optimization_barrier((grads, *held))
    received.update(zip(steps, held))
    for step in LATE:
        received[step] = shifted(received[step], "feat", step)
    grads = jnp.broadcast_to(grads[None], (plane, share, depth))
    grads = lax.all_to_all(grads, PLANE, split_axis=0, concat_axis=0, tiled=True)
    grads = grads.reshape(2 * depth, depth)
    feature_grad = place_step(pos, [received[step] for step in range(pieces)])
    return (feature_grad, grads[:depth], grads[depth:])


def solution(mesh):
    fine = Mesh(mesh.devices.reshape(2, 4, 4, 2, 8), RING)
    return jax.shard_map(
        on_device,
        mesh=fine,
        in_specs=(
            P("feat", DOM),
            P(DOM, None),
            P(DOM, None),
            P(DOM),
            P(DOM, None, None),
            P(),
            P(),
            P(None, RING),
        ),
        out_specs=(P("feat", DOM), P(), P()),
        check_vma=False,
    )
```

```python
import functools
import math

import jax
import jax.numpy as jnp
from jax import lax
from jax.experimental import pallas as pl
from jax.experimental.pallas import tpu as pltpu
from jax.sharding import Mesh, PartitionSpec as P

BLK = 128
REACH = 8
DOM = ("zh", "y", "x", "core")
PLANE = ("y", "x", "core")
LINE = ("zh", "feat")
RING = DOM + ("feat",)


def shifted(shard, axis, by):
    count = lax.axis_size(axis)
    return lax.ppermute(shard, axis, [(i, (i + by) % count) for i in range(count)])


def collected(rows):
    for axis in reversed(PLANE):
        count = lax.axis_size(axis)
        apart = 1
        while apart < count:
            other = lax.ppermute(rows, axis, [(i, i ^ apart) for i in range(count)])
            second = (lax.axis_index(axis) & apart) != 0
            rows = jnp.concatenate(
                [jnp.where(second, other, rows), jnp.where(second, rows, other)], axis=0
            )
            apart *= 2
    return rows


def tiles_of(width, tile):
    return [(at, min(tile, width - at)) for at in range(0, width, tile)]


def local_kernel(
    rows_ref,
    cols_ref,
    count_ref,
    pos_ref,
    own_ref,
    before_ref,
    after_ref,
    values_ref,
    w_in_ref,
    w_out_ref,
    cot_ref,
    middle_ref,
    left_ref,
    right_ref,
    stacked,
    delta,
    wide,
    agg,
    agg_grad,
    scat,
    sems,
):
    depth, width = own_ref.shape
    rim = before_ref.shape[1]
    chunk = width // BLK
    copies = [
        pltpu.make_async_copy(before_ref, wide.at[:, pl.ds(0, rim)], sems.at[0]),
        pltpu.make_async_copy(own_ref, wide.at[:, pl.ds(rim, width)], sems.at[1]),
        pltpu.make_async_copy(after_ref, wide.at[:, pl.ds(rim + width, rim)], sems.at[2]),
    ]
    for copy in copies:
        copy.start()
    agg[...] = jnp.zeros_like(agg)
    scat[:, :rim] = jnp.zeros((depth, rim), jnp.float32)
    scat[:, rim + width :] = jnp.zeros((depth, rim), jnp.float32)
    first = pos_ref[0] * chunk
    count = count_ref[0]
    for copy in copies:
        copy.wait()

    def gather_slot(slot, carry):
        row = rows_ref[slot] - first

        @pl.when((row >= 0) & (row < chunk))
        def _():
            col = cols_ref[slot] - first
            source = wide[:, pl.ds(pl.multiple_of(col * BLK, BLK), BLK)]
            into = pl.ds(pl.multiple_of(row * BLK, BLK), BLK)
            agg[:, into] += lax.dot_general(
                source,
                values_ref[slot],
                (((1,), (1,)), ((), ())),
                preferred_element_type=jnp.float32,
            )

        return carry

    lax.fori_loop(0, count, gather_slot, 0)

    for at, size in tiles_of(width, 256):
        part = slice(at, at + size)
        stacked[:depth, part] = wide[:, rim + at : rim + at + size]
        stacked[depth:, part] = agg[:, part].astype(jnp.bfloat16)
        preact = jnp.dot(w_in_ref[...], stacked[:, part], preferred_element_type=jnp.float32)
        sigma = 1.0 / (1.0 + jnp.exp(-preact))
        slope = sigma * (1.0 + preact * (1.0 - sigma))
        delta[:, part] = (cot_ref[:, part].astype(jnp.float32) * slope).astype(jnp.bfloat16)
        both = jnp.dot(w_out_ref[...], delta[:, part], preferred_element_type=jnp.float32)
        both = both.astype(jnp.bfloat16)
        scat[:, rim + at : rim + at + size] = both[:depth].astype(jnp.float32)
        agg_grad[:, part] = both[depth:]

    def scatter_slot(slot, carry):
        row = rows_ref[slot] - first

        @pl.when((row >= 0) & (row < chunk))
        def _():
            col = cols_ref[slot] - first
            source = agg_grad[:, pl.ds(pl.multiple_of(row * BLK, BLK), BLK)]
            into = pl.ds(pl.multiple_of(col * BLK, BLK), BLK)
            scat[:, into] += jnp.dot(
                source, values_ref[slot], preferred_element_type=jnp.float32
            )

        return carry

    lax.fori_loop(0, count, scatter_slot, 0)
    left_ref[...] = scat[:, :rim].astype(jnp.bfloat16)
    right_ref[...] = scat[:, rim + width :].astype(jnp.bfloat16)
    middle_ref[...] = scat[:, rim : rim + width]


def local_step(rows, cols, count, pos, own, before, after, values, w_in, w_out, cot):
    depth, width = own.shape
    rim = before.shape[1]
    smem = pl.BlockSpec(memory_space=pltpu.SMEM)
    vmem = pl.BlockSpec(memory_space=pltpu.VMEM)
    anywhere = pl.BlockSpec(memory_space=pl.ANY)
    return pl.pallas_call(
        local_kernel,
        out_shape=(
            jax.ShapeDtypeStruct((depth, width), jnp.float32),
            jax.ShapeDtypeStruct((depth, rim), jnp.bfloat16),
            jax.ShapeDtypeStruct((depth, rim), jnp.bfloat16),
            jax.ShapeDtypeStruct((2 * depth, width), jnp.bfloat16),
            jax.ShapeDtypeStruct((depth, width), jnp.bfloat16),
        ),
        in_specs=[smem] * 4 + [anywhere] * 3 + [vmem] * 4,
        out_specs=(vmem,) * 5,
        scratch_shapes=[
            pltpu.VMEM((depth, width + 2 * rim), jnp.bfloat16),
            pltpu.VMEM((depth, width), jnp.float32),
            pltpu.VMEM((depth, width), jnp.bfloat16),
            pltpu.VMEM((depth, width + 2 * rim), jnp.float32),
            pltpu.SemaphoreType.DMA((3,)),
        ],
        compiler_params=pltpu.CompilerParams(vmem_limit_bytes=48 * 1024 * 1024),
        cost_estimate=pl.CostEstimate(
            flops=12 * depth * depth * width, bytes_accessed=8 << 20, transcendentals=depth * width
        ),
    )(rows, cols, count, pos, own, before, after, values, w_in, w_out, cot)


def on_device(
    features, block_row, block_col, block_count, block_values, w_self, w_neigh, cotangent
):
    rows_part = features.shape[1]
    depth, width = cotangent.shape
    rim = REACH * BLK
    own = lax.all_to_all(features, "feat", split_axis=1, concat_axis=0, tiled=True)
    before = shifted(own[:, width - rim :], RING, 1)
    after = shifted(own[:, :rim], RING, -1)
    w_in = jnp.concatenate([w_self.T, w_neigh.T], axis=1)
    w_out = jnp.concatenate([w_self, w_neigh], axis=0)
    pos = lax.axis_index("feat").astype(jnp.int32)[None]
    middle, left, right, stacked, delta = local_step(
        block_row[0],
        block_col[0],
        block_count,
        pos,
        own,
        before,
        after,
        block_values,
        w_in,
        w_out,
        cotangent,
    )
    terms = jnp.einsum("in,on->io", stacked, delta, preferred_element_type=jnp.float32)
    plane, line = lax.axis_size(PLANE), lax.axis_size(LINE)
    share = 2 * depth // plane
    from_next = shifted(left, RING, -1)
    parts = lax.all_to_all(terms, PLANE, split_axis=0, concat_axis=0, tiled=True)
    partial = parts.reshape(plane, share, depth).sum(0)
    partial, from_next, right = lax.optimization_barrier((partial, from_next, right))
    from_prev = shifted(right, RING, 1)
    copies = jnp.broadcast_to(partial[None], (line, share, depth))
    copies = lax.all_to_all(copies, LINE, split_axis=0, concat_axis=0, tiled=True)
    factor = 1.0 / math.sqrt(rows_part * lax.axis_size(DOM))
    grads = (copies.reshape(line, share, depth).sum(0) * factor).astype(jnp.bfloat16)
    total = middle + jnp.pad(from_prev.astype(jnp.float32), ((0, 0), (0, width - rim)))
    total = total + jnp.pad(from_next.astype(jnp.float32), ((0, 0), (width - rim, 0)))
    total = total.astype(jnp.bfloat16)
    total, grads = lax.optimization_barrier((total, grads))
    feature_grad = lax.all_to_all(total, "feat", split_axis=0, concat_axis=1, tiled=True)
    grads = collected(grads)
    return (feature_grad, grads[:depth], grads[depth:])


def solution(mesh):
    fine = Mesh(mesh.devices.reshape(2, 4, 4, 2, 8), RING)
    return jax.shard_map(
        on_device,
        mesh=fine,
        in_specs=(
            P("feat", DOM),
            P(DOM, None),
            P(DOM, None),
            P(DOM),
            P(DOM, None, None),
            P(),
            P(),
            P(None, RING),
        ),
        out_specs=(P("feat", DOM), P(), P()),
        check_vma=False,
    )
```

```python
import functools
import math

import jax
import jax.numpy as jnp
from jax import lax
from jax.experimental import pallas as pl
from jax.experimental.pallas import tpu as pltpu
from jax.sharding import Mesh, PartitionSpec as P

BLK = 128
REACH = 8
DOM = ("zh", "y", "x", "core")
PLANE = ("y", "x", "core")
RING = DOM + ("feat",)


def shifted(shard, axis, by):
    count = lax.axis_size(axis)
    return lax.ppermute(shard, axis, [(i, (i + by) % count) for i in range(count)])


def collected(rows):
    for axis in reversed(PLANE):
        count = lax.axis_size(axis)
        apart = 1
        while apart < count:
            other = lax.ppermute(rows, axis, [(i, i ^ apart) for i in range(count)])
            second = (lax.axis_index(axis) & apart) != 0
            rows = jnp.concatenate(
                [jnp.where(second, other, rows), jnp.where(second, rows, other)], axis=0
            )
            apart *= 2
    return rows


def tiles_of(width, tile):
    return [(at, min(tile, width - at)) for at in range(0, width, tile)]


SMEM = pl.BlockSpec(memory_space=pltpu.SMEM)
VMEM = pl.BlockSpec(memory_space=pltpu.VMEM)
LEFT, OWN, RIGHT = range(3)


def list_kernel(chunk, rows_ref, cols_ref, count_ref, pos_ref, used_ref, slot_ref, row_ref, col_ref):
    slots = rows_ref.shape[0]
    first = pos_ref[0] * chunk
    for kind in range(3):
        used_ref[kind] = 0

    def step(slot, carry):
        row = rows_ref[slot] - first

        @pl.when((row >= 0) & (row < chunk))
        def _():
            col = cols_ref[slot] - first - REACH
            kind = jnp.where(col < 0, LEFT, jnp.where(col < chunk, OWN, RIGHT))
            base = jnp.where(col < 0, REACH, jnp.where(col < chunk, 0, -chunk))
            at = kind * slots + used_ref[kind]
            slot_ref[at] = slot
            row_ref[at] = row
            col_ref[at] = col + base
            used_ref[kind] = used_ref[kind] + 1

        return carry

    lax.fori_loop(0, jnp.minimum(count_ref[0], slots), step, 0)


def list_step(rows, cols, count, pos, chunk):
    table = jax.ShapeDtypeStruct((3 * rows.shape[0],), jnp.int32)
    return pl.pallas_call(
        functools.partial(list_kernel, chunk),
        out_shape=(jax.ShapeDtypeStruct((3,), jnp.int32), table, table, table),
        in_specs=[SMEM] * 4,
        out_specs=(SMEM,) * 4,
        cost_estimate=pl.CostEstimate(flops=0, bytes_accessed=4096, transcendentals=0),
    )(rows, cols, count, pos)


def block(index):
    return pl.ds(pl.multiple_of(index * BLK, BLK), BLK)


def add_slots(lists, kind, source, into, values, forward):
    used_ref, slot_ref, row_ref, col_ref = lists
    base = kind * (slot_ref.shape[0] // 3)
    count = used_ref[kind]

    def some(indices):
        products = []
        for at in indices:
            read = col_ref[at] if forward else row_ref[at]
            products.append(
                lax.dot_general(
                    source[:, block(read)],
                    values[slot_ref[at]],
                    (((1,), (1 if forward else 0,)), ((), ())),
                    preferred_element_type=jnp.float32,
                )
            )
        for at, product in zip(indices, products):
            write = row_ref[at] if forward else col_ref[at]
            into[:, block(write)] += product

    def pair(step, carry):
        some([base + 2 * step, base + 2 * step + 1])
        return carry

    lax.fori_loop(0, lax.div(count, 2), pair, 0)

    @pl.when(lax.rem(count, 2) == 1)
    def _():
        some([base + count - 1])


def before_kernel(*refs):
    lists, (own_ref, values_ref, agg_ref) = refs[:4], refs[4:]
    agg_ref[...] = jnp.zeros_like(agg_ref)
    add_slots(lists, OWN, own_ref, agg_ref, values_ref, True)


def before_step(lists, own, values):
    return pl.pallas_call(
        before_kernel,
        out_shape=jax.ShapeDtypeStruct(own.shape, jnp.float32),
        in_specs=[SMEM] * 4 + [VMEM] * 2,
        out_specs=VMEM,
        compiler_params=pltpu.CompilerParams(vmem_limit_bytes=24 * 1024 * 1024),
        cost_estimate=pl.CostEstimate(flops=1 << 28, bytes_accessed=4 << 20, transcendentals=0),
    )(*lists, own, values)


def local_kernel(*refs):
    lists = refs[:4]
    (agg_ref, own_ref, before_ref, after_ref, values_ref, w_in_ref, w_out_ref, cot_ref) = refs[4:12]
    left_ref, right_ref, stacked, delta, both_ref, agg, scat = refs[12:]
    depth, width = own_ref.shape
    agg[...] = agg_ref[...]
    add_slots(lists, LEFT, before_ref, agg, values_ref, True)
    add_slots(lists, RIGHT, after_ref, agg, values_ref, True)
    for at, size in tiles_of(width, 256):
        part = slice(at, at + size)
        stacked[:depth, part] = own_ref[:, part]
        stacked[depth:, part] = agg[:, part].astype(jnp.bfloat16)
        preact = jnp.dot(w_in_ref[...], stacked[:, part], preferred_element_type=jnp.float32)
        sigma = 1.0 / (1.0 + jnp.exp(-preact))
        slope = sigma * (1.0 + preact * (1.0 - sigma))
        delta[:, part] = (cot_ref[:, part].astype(jnp.float32) * slope).astype(jnp.bfloat16)
        both = jnp.dot(w_out_ref[...], delta[:, part], preferred_element_type=jnp.float32)
        both_ref[:, part] = both.astype(jnp.bfloat16)
    agg_grad = both_ref.at[pl.ds(depth, depth)]
    for kind, out_ref in ((LEFT, left_ref), (RIGHT, right_ref)):
        scat[...] = jnp.zeros_like(scat)
        add_slots(lists, kind, agg_grad, scat, values_ref, False)
        out_ref[...] = scat[...].astype(jnp.bfloat16)


def local_step(lists, agg, own, before, after, values, w_in, w_out, cot):
    depth, width = own.shape
    rim = before.shape[1]
    return pl.pallas_call(
        local_kernel,
        out_shape=(
            jax.ShapeDtypeStruct((depth, rim), jnp.bfloat16),
            jax.ShapeDtypeStruct((depth, rim), jnp.bfloat16),
            jax.ShapeDtypeStruct((2 * depth, width), jnp.bfloat16),
            jax.ShapeDtypeStruct((depth, width), jnp.bfloat16),
            jax.ShapeDtypeStruct((2 * depth, width), jnp.bfloat16),
        ),
        in_specs=[SMEM] * 4 + [VMEM] * 8,
        out_specs=(VMEM,) * 5,
        scratch_shapes=[
            pltpu.VMEM((depth, width), jnp.float32),
            pltpu.VMEM((depth, rim), jnp.float32),
        ],
        compiler_params=pltpu.CompilerParams(vmem_limit_bytes=40 * 1024 * 1024),
        cost_estimate=pl.CostEstimate(
            flops=12 * depth * depth * width, bytes_accessed=8 << 20, transcendentals=depth * width
        ),
    )(*lists, agg, own, before, after, values, w_in, w_out, cot)


def after_kernel(*refs):
    lists, (both_ref, values_ref, middle_ref) = refs[:4], refs[4:]
    depth = middle_ref.shape[0]
    middle_ref[...] = both_ref[:depth].astype(jnp.float32)
    add_slots(lists, OWN, both_ref.at[pl.ds(depth, depth)], middle_ref, values_ref, False)


def after_step(lists, both, values):
    return pl.pallas_call(
        after_kernel,
        out_shape=jax.ShapeDtypeStruct((both.shape[0] // 2, both.shape[1]), jnp.float32),
        in_specs=[SMEM] * 4 + [VMEM] * 2,
        out_specs=VMEM,
        compiler_params=pltpu.CompilerParams(vmem_limit_bytes=24 * 1024 * 1024),
        cost_estimate=pl.CostEstimate(flops=1 << 28, bytes_accessed=6 << 20, transcendentals=0),
    )(*lists, both, values)


def on_device(
    features, block_row, block_col, block_count, block_values, w_self, w_neigh, cotangent
):
    rows_part = features.shape[1]
    depth, width = cotangent.shape
    rim = REACH * BLK
    chunk = width // BLK
    pos = lax.axis_index("feat").astype(jnp.int32)[None]
    lists = list_step(block_row[0], block_col[0], block_count, pos, chunk)
    w_in = jnp.concatenate([w_self.T, w_neigh.T], axis=1)
    w_out = jnp.concatenate([w_self, w_neigh], axis=0)
    own = lax.all_to_all(features, "feat", split_axis=1, concat_axis=0, tiled=True)
    before = shifted(own[:, width - rim :], RING, 1)
    after = shifted(own[:, :rim], RING, -1)
    agg = before_step(lists, own, block_values)
    left, right, stacked, delta, both = local_step(
        lists, agg, own, before, after, block_values, w_in, w_out, cotangent
    )
    terms = jnp.einsum("in,on->io", stacked, delta, preferred_element_type=jnp.float32)
    plane, line = lax.axis_size(PLANE), lax.axis_size("feat")
    share = 2 * depth // plane
    from_next = shifted(left, RING, -1)
    parts = lax.all_to_all(terms, PLANE, split_axis=0, concat_axis=0, tiled=True)
    partial = parts.reshape(plane, share, depth).sum(0)
    partial, from_next, right, both = lax.optimization_barrier((partial, from_next, right, both))
    from_prev = shifted(right, RING, 1)
    middle = after_step(lists, both, block_values)
    copies = jnp.broadcast_to(partial[None], (line, share, depth))
    copies = lax.all_to_all(copies, "feat", split_axis=0, concat_axis=0, tiled=True)
    grads = copies.sum(0)
    total = middle + jnp.pad(from_prev.astype(jnp.float32), ((0, 0), (0, width - rim)))
    total = total + jnp.pad(from_next.astype(jnp.float32), ((0, 0), (width - rim, 0)))
    total = total.astype(jnp.bfloat16)
    total, grads = lax.optimization_barrier((total, grads))
    feature_grad = lax.all_to_all(total, "feat", split_axis=0, concat_axis=1, tiled=True)
    grads = grads + shifted(grads, "zh", 1)
    factor = 1.0 / math.sqrt(rows_part * lax.axis_size(DOM))
    grads = collected((grads * factor).astype(jnp.bfloat16))
    return (feature_grad, grads[:depth], grads[depth:])


def solution(mesh):
    fine = Mesh(mesh.devices.reshape(2, 4, 4, 2, 8), RING)
    return jax.shard_map(
        on_device,
        mesh=fine,
        in_specs=(
            P("feat", DOM),
            P(DOM, None),
            P(DOM, None),
            P(DOM),
            P(DOM, None, None),
            P(),
            P(),
            P(None, RING),
        ),
        out_specs=(P("feat", DOM), P(), P()),
        check_vma=False,
    )
```

```python
import functools
import math

import jax
import jax.numpy as jnp
from jax import lax
from jax.experimental import pallas as pl
from jax.experimental.pallas import tpu as pltpu
from jax.sharding import Mesh, PartitionSpec as P

BLK = 128
REACH = 8
DOM = ("zh", "y", "x", "core")
PLANE = ("y", "x", "core")
LINE = ("zh", "feat")
RING = DOM + ("feat",)


def shifted(shard, axis, by):
    count = lax.axis_size(axis)
    return lax.ppermute(shard, axis, [(i, (i + by) % count) for i in range(count)])


def collected(rows):
    for axis in reversed(PLANE):
        count = lax.axis_size(axis)
        apart = 1
        while apart < count:
            other = lax.ppermute(rows, axis, [(i, i ^ apart) for i in range(count)])
            second = (lax.axis_index(axis) & apart) != 0
            rows = jnp.concatenate(
                [jnp.where(second, other, rows), jnp.where(second, rows, other)], axis=0
            )
            apart *= 2
    return rows


def tiles_of(width, tile):
    return [(at, min(tile, width - at)) for at in range(0, width, tile)]


SMEM = pl.BlockSpec(memory_space=pltpu.SMEM)
VMEM = pl.BlockSpec(memory_space=pltpu.VMEM)
LEFT, OWN, RIGHT = range(3)


def list_kernel(chunk, rows_ref, cols_ref, count_ref, pos_ref, used_ref, slot_ref, row_ref, col_ref):
    slots = rows_ref.shape[0]
    first = pos_ref[0] * chunk
    for kind in range(3):
        used_ref[kind] = 0

    def step(slot, carry):
        row = rows_ref[slot] - first

        @pl.when((row >= 0) & (row < chunk))
        def _():
            col = cols_ref[slot] - first - REACH
            kind = jnp.where(col < 0, LEFT, jnp.where(col < chunk, OWN, RIGHT))
            base = jnp.where(col < 0, REACH, jnp.where(col < chunk, 0, -chunk))
            at = kind * slots + used_ref[kind]
            slot_ref[at] = slot
            row_ref[at] = row
            col_ref[at] = col + base
            used_ref[kind] = used_ref[kind] + 1

        return carry

    lax.fori_loop(0, jnp.minimum(count_ref[0], slots), step, 0)


def list_step(rows, cols, count, pos, chunk):
    table = jax.ShapeDtypeStruct((3 * rows.shape[0],), jnp.int32)
    return pl.pallas_call(
        functools.partial(list_kernel, chunk),
        out_shape=(jax.ShapeDtypeStruct((3,), jnp.int32), table, table, table),
        in_specs=[SMEM] * 4,
        out_specs=(SMEM,) * 4,
        cost_estimate=pl.CostEstimate(flops=0, bytes_accessed=4096, transcendentals=0),
    )(rows, cols, count, pos)


def block(index):
    return pl.ds(pl.multiple_of(index * BLK, BLK), BLK)


def add_slots(lists, kind, source, into, values, forward):
    used_ref, slot_ref, row_ref, col_ref = lists
    base = kind * (slot_ref.shape[0] // 3)
    count = used_ref[kind]

    def some(indices):
        products = []
        for at in indices:
            read = col_ref[at] if forward else row_ref[at]
            products.append(
                lax.dot_general(
                    source[:, block(read)],
                    values[slot_ref[at]],
                    (((1,), (1 if forward else 0,)), ((), ())),
                    preferred_element_type=jnp.float32,
                )
            )
        for at, product in zip(indices, products):
            write = row_ref[at] if forward else col_ref[at]
            into[:, block(write)] += product

    def pair(step, carry):
        some([base + 2 * step, base + 2 * step + 1])
        return carry

    lax.fori_loop(0, lax.div(count, 2), pair, 0)

    @pl.when(lax.rem(count, 2) == 1)
    def _():
        some([base + count - 1])


def before_kernel(*refs):
    lists, (own_ref, values_ref, agg_ref) = refs[:4], refs[4:]
    agg_ref[...] = jnp.zeros_like(agg_ref)
    add_slots(lists, OWN, own_ref, agg_ref, values_ref, True)


def before_step(lists, own, values):
    return pl.pallas_call(
        before_kernel,
        out_shape=jax.ShapeDtypeStruct(own.shape, jnp.float32),
        in_specs=[SMEM] * 4 + [VMEM] * 2,
        out_specs=VMEM,
        compiler_params=pltpu.CompilerParams(vmem_limit_bytes=24 * 1024 * 1024),
        cost_estimate=pl.CostEstimate(flops=1 << 28, bytes_accessed=4 << 20, transcendentals=0),
    )(*lists, own, values)


def local_kernel(*refs):
    lists = refs[:4]
    (agg_ref, own_ref, before_ref, after_ref, values_ref, w_in_ref, w_out_ref, cot_ref) = refs[4:12]
    left_ref, right_ref, stacked, delta, both_ref, agg, scat = refs[12:]
    depth, width = own_ref.shape
    agg[...] = agg_ref[...]
    add_slots(lists, LEFT, before_ref, agg, values_ref, True)
    add_slots(lists, RIGHT, after_ref, agg, values_ref, True)
    for at, size in tiles_of(width, 256):
        part = slice(at, at + size)
        stacked[:depth, part] = own_ref[:, part]
        stacked[depth:, part] = agg[:, part].astype(jnp.bfloat16)
        preact = jnp.dot(w_in_ref[...], stacked[:, part], preferred_element_type=jnp.float32)
        sigma = 1.0 / (1.0 + jnp.exp(-preact))
        slope = sigma * (1.0 + preact * (1.0 - sigma))
        delta[:, part] = (cot_ref[:, part].astype(jnp.float32) * slope).astype(jnp.bfloat16)
        both = jnp.dot(w_out_ref[...], delta[:, part], preferred_element_type=jnp.float32)
        both_ref[:, part] = both.astype(jnp.bfloat16)
    agg_grad = both_ref.at[pl.ds(depth, depth)]
    for kind, out_ref in ((LEFT, left_ref), (RIGHT, right_ref)):
        scat[...] = jnp.zeros_like(scat)
        add_slots(lists, kind, agg_grad, scat, values_ref, False)
        out_ref[...] = scat[...].astype(jnp.bfloat16)


def local_step(lists, agg, own, before, after, values, w_in, w_out, cot):
    depth, width = own.shape
    rim = before.shape[1]
    return pl.pallas_call(
        local_kernel,
        out_shape=(
            jax.ShapeDtypeStruct((depth, rim), jnp.bfloat16),
            jax.ShapeDtypeStruct((depth, rim), jnp.bfloat16),
            jax.ShapeDtypeStruct((2 * depth, width), jnp.bfloat16),
            jax.ShapeDtypeStruct((depth, width), jnp.bfloat16),
            jax.ShapeDtypeStruct((2 * depth, width), jnp.bfloat16),
        ),
        in_specs=[SMEM] * 4 + [VMEM] * 8,
        out_specs=(VMEM,) * 5,
        scratch_shapes=[
            pltpu.VMEM((depth, width), jnp.float32),
            pltpu.VMEM((depth, rim), jnp.float32),
        ],
        compiler_params=pltpu.CompilerParams(vmem_limit_bytes=40 * 1024 * 1024),
        cost_estimate=pl.CostEstimate(
            flops=12 * depth * depth * width, bytes_accessed=8 << 20, transcendentals=depth * width
        ),
    )(*lists, agg, own, before, after, values, w_in, w_out, cot)


def after_kernel(*refs):
    lists, (both_ref, values_ref, middle_ref) = refs[:4], refs[4:]
    depth = middle_ref.shape[0]
    middle_ref[...] = both_ref[:depth].astype(jnp.float32)
    add_slots(lists, OWN, both_ref.at[pl.ds(depth, depth)], middle_ref, values_ref, False)


def after_step(lists, both, values):
    return pl.pallas_call(
        after_kernel,
        out_shape=jax.ShapeDtypeStruct((both.shape[0] // 2, both.shape[1]), jnp.float32),
        in_specs=[SMEM] * 4 + [VMEM] * 2,
        out_specs=VMEM,
        compiler_params=pltpu.CompilerParams(vmem_limit_bytes=24 * 1024 * 1024),
        cost_estimate=pl.CostEstimate(flops=1 << 28, bytes_accessed=6 << 20, transcendentals=0),
    )(*lists, both, values)


def total_kernel(middle_ref, prev_ref, next_ref, out_ref):
    width, rim = middle_ref.shape[1], prev_ref.shape[1]
    edges = sorted({0, min(rim, width - rim), max(rim, width - rim), width})
    for at, end in zip(edges, edges[1:]):
        part = middle_ref[:, at:end]
        if at < rim:
            part = part + prev_ref[:, at:end].astype(jnp.float32)
        if at >= width - rim:
            here = at - (width - rim)
            part = part + next_ref[:, here : here + end - at].astype(jnp.float32)
        out_ref[:, at:end] = part.astype(jnp.bfloat16)


def total_step(middle, from_prev, from_next):
    return pl.pallas_call(
        total_kernel,
        out_shape=jax.ShapeDtypeStruct(middle.shape, jnp.bfloat16),
        in_specs=[VMEM] * 3,
        out_specs=VMEM,
        compiler_params=pltpu.CompilerParams(vmem_limit_bytes=24 * 1024 * 1024),
        cost_estimate=pl.CostEstimate(flops=0, bytes_accessed=4 << 20, transcendentals=0),
    )(middle, from_prev, from_next)


def on_device(
    features, block_row, block_col, block_count, block_values, w_self, w_neigh, cotangent
):
    rows_part = features.shape[1]
    depth, width = cotangent.shape
    rim = REACH * BLK
    chunk = width // BLK
    pos = lax.axis_index("feat").astype(jnp.int32)[None]
    lists = list_step(block_row[0], block_col[0], block_count, pos, chunk)
    w_in = jnp.concatenate([w_self.T, w_neigh.T], axis=1)
    w_out = jnp.concatenate([w_self, w_neigh], axis=0)
    own = lax.all_to_all(features, "feat", split_axis=1, concat_axis=0, tiled=True)
    before = shifted(own[:, width - rim :], RING, 1)
    after = shifted(own[:, :rim], RING, -1)
    agg = before_step(lists, own, block_values)
    left, right, stacked, delta, both = local_step(
        lists, agg, own, before, after, block_values, w_in, w_out, cotangent
    )
    terms = jnp.einsum("in,on->io", stacked, delta, preferred_element_type=jnp.float32)
    plane, line = lax.axis_size(PLANE), lax.axis_size(LINE)
    share = 2 * depth // plane
    from_next = shifted(left, RING, -1)
    from_prev = shifted(right, RING, 1)
    parts = lax.all_to_all(terms, PLANE, split_axis=0, concat_axis=0, tiled=True)
    partial = parts.reshape(plane, share, depth).sum(0).astype(jnp.bfloat16)
    partial, from_next, from_prev, used = lax.optimization_barrier(
        (partial, from_next, from_prev, lists[0])
    )
    middle = after_step([used, *lists[1:]], both, block_values)
    copies = jnp.broadcast_to(partial[None], (line, share, depth))
    copies = lax.all_to_all(copies, LINE, split_axis=0, concat_axis=0, tiled=True)
    factor = 1.0 / math.sqrt(rows_part * lax.axis_size(DOM))
    grads = copies.reshape(line, share, depth).astype(jnp.float32).sum(0) * factor
    total = total_step(middle, from_prev, from_next)
    total, grads = lax.optimization_barrier((total, grads.astype(jnp.bfloat16)))
    feature_grad = lax.all_to_all(total, "feat", split_axis=0, concat_axis=1, tiled=True)
    grads = collected(grads)
    return (feature_grad, grads[:depth], grads[depth:])


def solution(mesh):
    fine = Mesh(mesh.devices.reshape(2, 4, 4, 2, 8), RING)
    return jax.shard_map(
        on_device,
        mesh=fine,
        in_specs=(
            P("feat", DOM),
            P(DOM, None),
            P(DOM, None),
            P(DOM),
            P(DOM, None, None),
            P(),
            P(),
            P(None, RING),
        ),
        out_specs=(P("feat", DOM), P(), P()),
        check_vma=False,
    )
```

```python
import functools
import math

import jax
import jax.numpy as jnp
from jax import lax
from jax.experimental import pallas as pl
from jax.experimental.pallas import tpu as pltpu
from jax.sharding import Mesh, PartitionSpec as P

BLK = 128
REACH = 8
DOM = ("zh", "y", "x", "core")
PLANE = ("y", "x", "core")
LINE = ("zh", "feat")
RING = DOM + ("feat",)


def shifted(shard, axis, by):
    count = lax.axis_size(axis)
    return lax.ppermute(shard, axis, [(i, (i + by) % count) for i in range(count)])


def collected(rows):
    for axis in reversed(PLANE):
        count = lax.axis_size(axis)
        apart = 1
        while apart < count:
            other = lax.ppermute(rows, axis, [(i, i ^ apart) for i in range(count)])
            second = (lax.axis_index(axis) & apart) != 0
            rows = jnp.concatenate(
                [jnp.where(second, other, rows), jnp.where(second, rows, other)], axis=0
            )
            apart *= 2
    return rows


def tiles_of(width, tile):
    return [(at, min(tile, width - at)) for at in range(0, width, tile)]


SMEM = pl.BlockSpec(memory_space=pltpu.SMEM)
VMEM = pl.BlockSpec(memory_space=pltpu.VMEM)
HBM = pl.BlockSpec(memory_space=pltpu.HBM)
LEFT, OWN, RIGHT = range(3)


def list_kernel(chunk, rows_ref, cols_ref, count_ref, pos_ref, used_ref, slot_ref, row_ref, col_ref):
    slots = rows_ref.shape[0]
    first = pos_ref[0] * chunk
    for kind in range(3):
        used_ref[kind] = 0

    def step(slot, carry):
        row = rows_ref[slot] - first

        @pl.when((row >= 0) & (row < chunk))
        def _():
            col = cols_ref[slot] - first - REACH
            kind = jnp.where(col < 0, LEFT, jnp.where(col < chunk, OWN, RIGHT))
            base = jnp.where(col < 0, REACH, jnp.where(col < chunk, 0, -chunk))
            at = kind * slots + used_ref[kind]
            slot_ref[at] = slot
            row_ref[at] = row
            col_ref[at] = col + base
            used_ref[kind] = used_ref[kind] + 1

        return carry

    lax.fori_loop(0, jnp.minimum(count_ref[0], slots), step, 0)


def list_step(rows, cols, count, pos, chunk):
    table = jax.ShapeDtypeStruct((3 * rows.shape[0],), jnp.int32)
    return pl.pallas_call(
        functools.partial(list_kernel, chunk),
        out_shape=(jax.ShapeDtypeStruct((3,), jnp.int32), table, table, table),
        in_specs=[SMEM] * 4,
        out_specs=(SMEM,) * 4,
        cost_estimate=pl.CostEstimate(flops=0, bytes_accessed=4096, transcendentals=0),
    )(rows, cols, count, pos)


def block(index):
    return pl.ds(pl.multiple_of(index * BLK, BLK), BLK)


def add_slots(lists, kind, source, into, values, forward):
    used_ref, slot_ref, row_ref, col_ref = lists
    base = kind * (slot_ref.shape[0] // 3)
    count = used_ref[kind]

    def some(indices):
        products = []
        for at in indices:
            read = col_ref[at] if forward else row_ref[at]
            products.append(
                lax.dot_general(
                    source[:, block(read)],
                    values[slot_ref[at]],
                    (((1,), (1 if forward else 0,)), ((), ())),
                    preferred_element_type=jnp.float32,
                )
            )
        for at, product in zip(indices, products):
            write = row_ref[at] if forward else col_ref[at]
            into[:, block(write)] += product

    def pair(step, carry):
        some([base + 2 * step, base + 2 * step + 1])
        return carry

    lax.fori_loop(0, lax.div(count, 2), pair, 0)

    @pl.when(lax.rem(count, 2) == 1)
    def _():
        some([base + count - 1])


def before_kernel(*refs):
    lists, (own_ref, values_ref, agg_ref) = refs[:4], refs[4:]
    agg_ref[...] = jnp.zeros_like(agg_ref)
    add_slots(lists, OWN, own_ref, agg_ref, values_ref, True)


def before_step(lists, own, values):
    return pl.pallas_call(
        before_kernel,
        out_shape=jax.ShapeDtypeStruct(own.shape, jnp.float32),
        in_specs=[SMEM] * 4 + [VMEM] * 2,
        out_specs=VMEM,
        compiler_params=pltpu.CompilerParams(vmem_limit_bytes=24 * 1024 * 1024),
        cost_estimate=pl.CostEstimate(flops=1 << 28, bytes_accessed=4 << 20, transcendentals=0),
    )(*lists, own, values)


def local_kernel(*refs):
    lists = refs[:4]
    (agg_ref, own_ref, before_ref, after_ref, values_ref, w_in_ref, w_out_ref, cot_ref) = refs[4:12]
    terms_ref, both_ref, stacked, delta, agg, held, terms, sems = refs[12:]
    depth, width = own_ref.shape
    agg[...] = agg_ref[...]
    add_slots(lists, LEFT, before_ref, agg, values_ref, True)
    add_slots(lists, RIGHT, after_ref, agg, values_ref, True)
    for at, size in tiles_of(width, 256):
        part = slice(at, at + size)
        stacked[:depth, part] = own_ref[:, part]
        stacked[depth:, part] = agg[:, part].astype(jnp.bfloat16)
        preact = jnp.dot(w_in_ref[...], stacked[:, part], preferred_element_type=jnp.float32)
        sigma = 1.0 / (1.0 + jnp.exp(-preact))
        slope = sigma * (1.0 + preact * (1.0 - sigma))
        delta[:, part] = (cot_ref[:, part].astype(jnp.float32) * slope).astype(jnp.bfloat16)
        both = jnp.dot(w_out_ref[...], delta[:, part], preferred_element_type=jnp.float32)
        held[:, part] = both.astype(jnp.bfloat16)
    first = pltpu.make_async_copy(held, both_ref, sems.at[0])
    first.start()
    terms[...] = lax.dot_general(
        stacked[...], delta[...], (((1,), (1,)), ((), ())), preferred_element_type=jnp.float32
    )
    second = pltpu.make_async_copy(terms, terms_ref, sems.at[1])
    second.start()
    first.wait()
    second.wait()


def edge_kernel(*refs):
    lists, (both_ref, values_ref, left_ref, right_ref, agg_grad, scat, sem) = refs[:4], refs[4:]
    depth = left_ref.shape[0]
    fetch = pltpu.make_async_copy(both_ref.at[pl.ds(depth, depth)], agg_grad, sem)
    fetch.start()
    fetch.wait()
    for kind, out_ref in ((LEFT, left_ref), (RIGHT, right_ref)):
        scat[...] = jnp.zeros_like(scat)
        add_slots(lists, kind, agg_grad, scat, values_ref, False)
        out_ref[...] = scat[...].astype(jnp.bfloat16)


def edge_step(lists, both, values, rim):
    depth, width = both.shape[0] // 2, both.shape[1]
    return pl.pallas_call(
        edge_kernel,
        out_shape=(jax.ShapeDtypeStruct((depth, rim), jnp.bfloat16),) * 2,
        in_specs=[SMEM] * 4 + [HBM, VMEM],
        out_specs=(VMEM,) * 2,
        scratch_shapes=[
            pltpu.VMEM((depth, width), jnp.bfloat16),
            pltpu.VMEM((depth, rim), jnp.float32),
            pltpu.SemaphoreType.DMA,
        ],
        compiler_params=pltpu.CompilerParams(vmem_limit_bytes=24 * 1024 * 1024),
        cost_estimate=pl.CostEstimate(flops=1 << 28, bytes_accessed=4 << 20, transcendentals=0),
    )(*lists, both, values)


def local_step(lists, agg, own, before, after, values, w_in, w_out, cot):
    depth, width = own.shape
    both = jax.ShapeDtypeStruct((2 * depth, width), jnp.bfloat16)
    return pl.pallas_call(
        local_kernel,
        out_shape=(jax.ShapeDtypeStruct((2 * depth, depth), jnp.float32), both),
        in_specs=[SMEM] * 4 + [VMEM] * 8,
        out_specs=(HBM, HBM),
        scratch_shapes=[
            pltpu.VMEM((2 * depth, width), jnp.bfloat16),
            pltpu.VMEM((depth, width), jnp.bfloat16),
            pltpu.VMEM((depth, width), jnp.float32),
            pltpu.VMEM((2 * depth, width), jnp.bfloat16),
            pltpu.VMEM((2 * depth, depth), jnp.float32),
            pltpu.SemaphoreType.DMA((2,)),
        ],
        compiler_params=pltpu.CompilerParams(vmem_limit_bytes=40 * 1024 * 1024),
        cost_estimate=pl.CostEstimate(
            flops=12 * depth * depth * width, bytes_accessed=8 << 20, transcendentals=depth * width
        ),
    )(*lists, agg, own, before, after, values, w_in, w_out, cot)


def after_kernel(*refs):
    lists, (both_ref, values_ref, middle_ref) = refs[:4], refs[4:]
    depth = middle_ref.shape[0]
    middle_ref[...] = both_ref[:depth].astype(jnp.float32)
    add_slots(lists, OWN, both_ref.at[pl.ds(depth, depth)], middle_ref, values_ref, False)


def after_step(lists, both, values):
    return pl.pallas_call(
        after_kernel,
        out_shape=jax.ShapeDtypeStruct((both.shape[0] // 2, both.shape[1]), jnp.float32),
        in_specs=[SMEM] * 4 + [VMEM] * 2,
        out_specs=VMEM,
        compiler_params=pltpu.CompilerParams(vmem_limit_bytes=24 * 1024 * 1024),
        cost_estimate=pl.CostEstimate(flops=1 << 28, bytes_accessed=6 << 20, transcendentals=0),
    )(*lists, both, values)


def total_kernel(middle_ref, prev_ref, next_ref, out_ref):
    width, rim = middle_ref.shape[1], prev_ref.shape[1]
    edges = sorted({0, min(rim, width - rim), max(rim, width - rim), width})
    for at, end in zip(edges, edges[1:]):
        part = middle_ref[:, at:end]
        if at < rim:
            part = part + prev_ref[:, at:end].astype(jnp.float32)
        if at >= width - rim:
            here = at - (width - rim)
            part = part + next_ref[:, here : here + end - at].astype(jnp.float32)
        out_ref[:, at:end] = part.astype(jnp.bfloat16)


def total_step(middle, from_prev, from_next):
    return pl.pallas_call(
        total_kernel,
        out_shape=jax.ShapeDtypeStruct(middle.shape, jnp.bfloat16),
        in_specs=[VMEM] * 3,
        out_specs=VMEM,
        compiler_params=pltpu.CompilerParams(vmem_limit_bytes=24 * 1024 * 1024),
        cost_estimate=pl.CostEstimate(flops=0, bytes_accessed=4 << 20, transcendentals=0),
    )(middle, from_prev, from_next)


def on_device(
    features, block_row, block_col, block_count, block_values, w_self, w_neigh, cotangent
):
    rows_part = features.shape[1]
    depth, width = cotangent.shape
    rim = REACH * BLK
    chunk = width // BLK
    pos = lax.axis_index("feat").astype(jnp.int32)[None]
    lists = list_step(block_row[0], block_col[0], block_count, pos, chunk)
    w_in = jnp.concatenate([w_self.T, w_neigh.T], axis=1)
    w_out = jnp.concatenate([w_self, w_neigh], axis=0)
    own = lax.all_to_all(features, "feat", split_axis=1, concat_axis=0, tiled=True)
    before = shifted(own[:, width - rim :], RING, 1)
    after = shifted(own[:, :rim], RING, -1)
    agg = before_step(lists, own, block_values)
    terms, both = local_step(
        lists, agg, own, before, after, block_values, w_in, w_out, cotangent
    )
    plane, line = lax.axis_size(PLANE), lax.axis_size(LINE)
    share = 2 * depth // plane
    used, terms = lax.optimization_barrier((lists[0], terms))
    left, right = edge_step([used, *lists[1:]], both, block_values, rim)
    from_next = shifted(left, RING, -1)
    from_prev = shifted(right, RING, 1)
    parts = lax.all_to_all(terms, PLANE, split_axis=0, concat_axis=0, tiled=True)
    partial = parts.reshape(plane, share, depth).sum(0).astype(jnp.bfloat16)
    partial, used = lax.optimization_barrier((partial, used))
    middle = after_step([used, *lists[1:]], both, block_values)
    copies = jnp.broadcast_to(partial[None], (line, share, depth))
    copies = lax.all_to_all(copies, LINE, split_axis=0, concat_axis=0, tiled=True)
    factor = 1.0 / math.sqrt(rows_part * lax.axis_size(DOM))
    grads = copies.reshape(line, share, depth).astype(jnp.float32).sum(0) * factor
    total = total_step(middle, from_prev, from_next)
    total, grads = lax.optimization_barrier((total, grads.astype(jnp.bfloat16)))
    feature_grad = lax.all_to_all(total, "feat", split_axis=0, concat_axis=1, tiled=True)
    grads = collected(grads)
    return (feature_grad, grads[:depth], grads[depth:])


def solution(mesh):
    fine = Mesh(mesh.devices.reshape(2, 4, 4, 2, 8), RING)
    return jax.shard_map(
        on_device,
        mesh=fine,
        in_specs=(
            P("feat", DOM),
            P(DOM, None),
            P(DOM, None),
            P(DOM),
            P(DOM, None, None),
            P(),
            P(),
            P(None, RING),
        ),
        out_specs=(P("feat", DOM), P(), P()),
        check_vma=False,
    )
```

```python
import functools
import math

import jax
import jax.numpy as jnp
from jax import lax
from jax.experimental import pallas as pl
from jax.experimental.pallas import tpu as pltpu
from jax.sharding import Mesh, PartitionSpec as P

BLK = 128
REACH = 8
DOM = ("zh", "y", "x", "core")
PLANE = ("y", "x", "core")
LINE = ("zh", "feat")
RING = DOM + ("feat",)


def shifted(shard, axis, by):
    count = lax.axis_size(axis)
    return lax.ppermute(shard, axis, [(i, (i + by) % count) for i in range(count)])


def collected(rows):
    for axis in reversed(PLANE):
        count = lax.axis_size(axis)
        apart = 1
        while apart < count:
            other = lax.ppermute(rows, axis, [(i, i ^ apart) for i in range(count)])
            second = (lax.axis_index(axis) & apart) != 0
            rows = jnp.concatenate(
                [jnp.where(second, other, rows), jnp.where(second, rows, other)], axis=0
            )
            apart *= 2
    return rows


def tiles_of(width, tile):
    return [(at, min(tile, width - at)) for at in range(0, width, tile)]


SMEM = pl.BlockSpec(memory_space=pltpu.SMEM)
VMEM = pl.BlockSpec(memory_space=pltpu.VMEM)
HBM = pl.BlockSpec(memory_space=pltpu.HBM)
LEFT, OWN, RIGHT = range(3)


def list_kernel(chunk, rows_ref, cols_ref, count_ref, pos_ref, used_ref, slot_ref, row_ref, col_ref):
    slots = rows_ref.shape[0]
    first = pos_ref[0] * chunk
    for kind in range(3):
        used_ref[kind] = 0

    def step(slot, carry):
        row = rows_ref[slot] - first

        @pl.when((row >= 0) & (row < chunk))
        def _():
            col = cols_ref[slot] - first - REACH
            kind = jnp.where(col < 0, LEFT, jnp.where(col < chunk, OWN, RIGHT))
            base = jnp.where(col < 0, REACH, jnp.where(col < chunk, 0, -chunk))
            at = kind * slots + used_ref[kind]
            slot_ref[at] = slot
            row_ref[at] = row
            col_ref[at] = col + base
            used_ref[kind] = used_ref[kind] + 1

        return carry

    lax.fori_loop(0, jnp.minimum(count_ref[0], slots), step, 0)


def list_step(rows, cols, count, pos, chunk):
    table = jax.ShapeDtypeStruct((3 * rows.shape[0],), jnp.int32)
    return pl.pallas_call(
        functools.partial(list_kernel, chunk),
        out_shape=(jax.ShapeDtypeStruct((3,), jnp.int32), table, table, table),
        in_specs=[SMEM] * 4,
        out_specs=(SMEM,) * 4,
        cost_estimate=pl.CostEstimate(flops=0, bytes_accessed=4096, transcendentals=0),
    )(rows, cols, count, pos)


def block(index):
    return pl.ds(pl.multiple_of(index * BLK, BLK), BLK)


def add_slots(lists, kind, source, into, values, forward):
    used_ref, slot_ref, row_ref, col_ref = lists
    base = kind * (slot_ref.shape[0] // 3)
    count = used_ref[kind]

    def some(indices):
        products = []
        for at in indices:
            read = col_ref[at] if forward else row_ref[at]
            products.append(
                lax.dot_general(
                    source[:, block(read)],
                    values[slot_ref[at]],
                    (((1,), (1 if forward else 0,)), ((), ())),
                    preferred_element_type=jnp.float32,
                )
            )
        for at, product in zip(indices, products):
            write = row_ref[at] if forward else col_ref[at]
            into[:, block(write)] += product

    def pair(step, carry):
        some([base + 2 * step, base + 2 * step + 1])
        return carry

    lax.fori_loop(0, lax.div(count, 2), pair, 0)

    @pl.when(lax.rem(count, 2) == 1)
    def _():
        some([base + count - 1])


def before_kernel(*refs):
    lists, (own_ref, values_ref, agg_ref) = refs[:4], refs[4:]
    agg_ref[...] = jnp.zeros_like(agg_ref)
    add_slots(lists, OWN, own_ref, agg_ref, values_ref, True)


def before_step(lists, own, values):
    return pl.pallas_call(
        before_kernel,
        out_shape=jax.ShapeDtypeStruct(own.shape, jnp.float32),
        in_specs=[SMEM] * 4 + [VMEM] * 2,
        out_specs=VMEM,
        compiler_params=pltpu.CompilerParams(vmem_limit_bytes=24 * 1024 * 1024),
        cost_estimate=pl.CostEstimate(flops=1 << 28, bytes_accessed=4 << 20, transcendentals=0),
    )(*lists, own, values)


def local_kernel(*refs):
    lists = refs[:4]
    (agg_ref, own_ref, before_ref, after_ref, values_ref, w_in_ref, w_out_ref, cot_ref) = refs[4:12]
    terms_ref, both_ref, stacked, delta, agg, held, terms, sems = refs[12:]
    depth, width = own_ref.shape
    agg[...] = agg_ref[...]
    add_slots(lists, LEFT, before_ref, agg, values_ref, True)
    add_slots(lists, RIGHT, after_ref, agg, values_ref, True)
    for at, size in tiles_of(width, 256):
        part = slice(at, at + size)
        stacked[:depth, part] = own_ref[:, part]
        stacked[depth:, part] = agg[:, part].astype(jnp.bfloat16)
        preact = jnp.dot(w_in_ref[...], stacked[:, part], preferred_element_type=jnp.float32)
        sigma = 1.0 / (1.0 + jnp.exp(-preact))
        slope = sigma * (1.0 + preact * (1.0 - sigma))
        delta[:, part] = (cot_ref[:, part].astype(jnp.float32) * slope).astype(jnp.bfloat16)
        both = jnp.dot(w_out_ref[...], delta[:, part], preferred_element_type=jnp.float32)
        held[:, part] = both.astype(jnp.bfloat16)
    first = pltpu.make_async_copy(held, both_ref, sems.at[0])
    first.start()
    terms[...] = lax.dot_general(
        stacked[...], delta[...], (((1,), (1,)), ((), ())), preferred_element_type=jnp.float32
    )
    second = pltpu.make_async_copy(terms, terms_ref, sems.at[1])
    second.start()
    first.wait()
    second.wait()


def edge_kernel(*refs):
    lists, (both_ref, values_ref, left_ref, right_ref, agg_grad, scat, sem) = refs[:4], refs[4:]
    depth = left_ref.shape[0]
    fetch = pltpu.make_async_copy(both_ref.at[pl.ds(depth, depth)], agg_grad, sem)
    fetch.start()
    fetch.wait()
    for kind, out_ref in ((LEFT, left_ref), (RIGHT, right_ref)):
        scat[...] = jnp.zeros_like(scat)
        add_slots(lists, kind, agg_grad, scat, values_ref, False)
        out_ref[...] = scat[...].astype(jnp.bfloat16)


def edge_step(lists, both, values, rim):
    depth, width = both.shape[0] // 2, both.shape[1]
    return pl.pallas_call(
        edge_kernel,
        out_shape=(jax.ShapeDtypeStruct((depth, rim), jnp.bfloat16),) * 2,
        in_specs=[SMEM] * 4 + [HBM, VMEM],
        out_specs=(VMEM,) * 2,
        scratch_shapes=[
            pltpu.VMEM((depth, width), jnp.bfloat16),
            pltpu.VMEM((depth, rim), jnp.float32),
            pltpu.SemaphoreType.DMA,
        ],
        compiler_params=pltpu.CompilerParams(vmem_limit_bytes=24 * 1024 * 1024),
        cost_estimate=pl.CostEstimate(flops=1 << 28, bytes_accessed=4 << 20, transcendentals=0),
    )(*lists, both, values)


def local_step(lists, agg, own, before, after, values, w_in, w_out, cot):
    depth, width = own.shape
    both = jax.ShapeDtypeStruct((2 * depth, width), jnp.bfloat16)
    return pl.pallas_call(
        local_kernel,
        out_shape=(jax.ShapeDtypeStruct((2 * depth, depth), jnp.float32), both),
        in_specs=[SMEM] * 4 + [VMEM] * 8,
        out_specs=(HBM, HBM),
        scratch_shapes=[
            pltpu.VMEM((2 * depth, width), jnp.bfloat16),
            pltpu.VMEM((depth, width), jnp.bfloat16),
            pltpu.VMEM((depth, width), jnp.float32),
            pltpu.VMEM((2 * depth, width), jnp.bfloat16),
            pltpu.VMEM((2 * depth, depth), jnp.float32),
            pltpu.SemaphoreType.DMA((2,)),
        ],
        compiler_params=pltpu.CompilerParams(vmem_limit_bytes=40 * 1024 * 1024),
        cost_estimate=pl.CostEstimate(
            flops=12 * depth * depth * width, bytes_accessed=8 << 20, transcendentals=depth * width
        ),
    )(*lists, agg, own, before, after, values, w_in, w_out, cot)


def after_kernel(*refs):
    lists, (both_ref, values_ref, middle_ref) = refs[:4], refs[4:]
    depth = middle_ref.shape[0]
    middle_ref[...] = both_ref[:depth].astype(jnp.float32)
    add_slots(lists, OWN, both_ref.at[pl.ds(depth, depth)], middle_ref, values_ref, False)


def after_step(lists, both, values):
    return pl.pallas_call(
        after_kernel,
        out_shape=jax.ShapeDtypeStruct((both.shape[0] // 2, both.shape[1]), jnp.float32),
        in_specs=[SMEM] * 4 + [VMEM] * 2,
        out_specs=VMEM,
        compiler_params=pltpu.CompilerParams(vmem_limit_bytes=24 * 1024 * 1024),
        cost_estimate=pl.CostEstimate(flops=1 << 28, bytes_accessed=6 << 20, transcendentals=0),
    )(*lists, both, values)


def total_kernel(middle_ref, prev_ref, next_ref, out_ref):
    width, rim = middle_ref.shape[1], prev_ref.shape[1]
    edges = sorted({0, min(rim, width - rim), max(rim, width - rim), width})
    for at, end in zip(edges, edges[1:]):
        part = middle_ref[:, at:end]
        if at < rim:
            part = part + prev_ref[:, at:end].astype(jnp.float32)
        if at >= width - rim:
            here = at - (width - rim)
            part = part + next_ref[:, here : here + end - at].astype(jnp.float32)
        out_ref[:, at:end] = part.astype(jnp.bfloat16)


def total_step(middle, from_prev, from_next):
    return pl.pallas_call(
        total_kernel,
        out_shape=jax.ShapeDtypeStruct(middle.shape, jnp.bfloat16),
        in_specs=[VMEM] * 3,
        out_specs=VMEM,
        compiler_params=pltpu.CompilerParams(vmem_limit_bytes=24 * 1024 * 1024),
        cost_estimate=pl.CostEstimate(flops=0, bytes_accessed=4 << 20, transcendentals=0),
    )(middle, from_prev, from_next)


def cut_kernel(pos_ref, features_ref, *refs):
    piece_refs, sems = refs[:-1], refs[-1]
    pieces, width = len(piece_refs), piece_refs[0].shape[1]
    copies = []
    for step, piece_ref in enumerate(piece_refs):
        dest = lax.rem(pos_ref[0] + step, pieces)
        part = pl.ds(pl.multiple_of(dest * width, BLK), width)
        copies.append(pltpu.make_async_copy(features_ref.at[:, part], piece_ref, sems.at[step]))
    for copy in copies:
        copy.start()
    for copy in copies:
        copy.wait()


def cut_step(pos, features, pieces):
    height, width = features.shape[0], features.shape[1] // pieces
    return pl.pallas_call(
        cut_kernel,
        out_shape=(jax.ShapeDtypeStruct((height, width), features.dtype),) * pieces,
        in_specs=[SMEM, pl.BlockSpec(memory_space=pl.ANY)],
        out_specs=(VMEM,) * pieces,
        scratch_shapes=[pltpu.SemaphoreType.DMA((pieces,))],
        compiler_params=pltpu.CompilerParams(vmem_limit_bytes=16 * 1024 * 1024),
        cost_estimate=pl.CostEstimate(flops=0, bytes_accessed=2 << 20, transcendentals=0),
    )(pos, features)


def join_kernel(pos_ref, *refs):
    piece_refs, (own_ref, head_ref, tail_ref) = refs[:-3], refs[-3:]
    pieces = len(piece_refs)
    height, width = piece_refs[0].shape
    rim = head_ref.shape[1]
    for step, piece_ref in enumerate(piece_refs):
        source = lax.rem(pos_ref[0] + pieces - step, pieces)
        rows = pl.ds(pl.multiple_of(source * height, height), height)
        own_ref[rows, :] = piece_ref[...]
        head_ref[rows, :] = piece_ref[:, :rim]
        tail_ref[rows, :] = piece_ref[:, width - rim :]


def join_step(pos, received, rim):
    pieces = len(received)
    height, width = received[0].shape
    depth, kind = pieces * height, received[0].dtype
    edge = jax.ShapeDtypeStruct((depth, rim), kind)
    return pl.pallas_call(
        join_kernel,
        out_shape=(jax.ShapeDtypeStruct((depth, width), kind), edge, edge),
        in_specs=[SMEM] + [VMEM] * pieces,
        out_specs=(VMEM,) * 3,
        compiler_params=pltpu.CompilerParams(vmem_limit_bytes=16 * 1024 * 1024),
        cost_estimate=pl.CostEstimate(flops=0, bytes_accessed=4 << 20, transcendentals=0),
    )(pos, *received)


def on_device(
    features, block_row, block_col, block_count, block_values, w_self, w_neigh, cotangent
):
    rows_part = features.shape[1]
    depth, width = cotangent.shape
    rim = REACH * BLK
    chunk = width // BLK
    pos = lax.axis_index("feat").astype(jnp.int32)[None]
    lists = list_step(block_row[0], block_col[0], block_count, pos, chunk)
    w_in = jnp.concatenate([w_self.T, w_neigh.T], axis=1)
    w_out = jnp.concatenate([w_self, w_neigh], axis=0)
    pieces = lax.axis_size("feat")
    received = list(cut_step(pos, features, pieces))
    for step in sorted(range(1, pieces), key=lambda step: (abs(2 * step - pieces), step)):
        received[step] = shifted(received[step], "feat", step)
    own, head, tail = join_step(pos, received, rim)
    before = shifted(tail, RING, 1)
    after = shifted(head, RING, -1)
    agg = before_step(lists, own, block_values)
    terms, both = local_step(
        lists, agg, own, before, after, block_values, w_in, w_out, cotangent
    )
    plane, line = lax.axis_size(PLANE), lax.axis_size(LINE)
    share = 2 * depth // plane
    used, terms = lax.optimization_barrier((lists[0], terms))
    left, right = edge_step([used, *lists[1:]], both, block_values, rim)
    from_next = shifted(left, RING, -1)
    from_prev = shifted(right, RING, 1)
    parts = lax.all_to_all(terms, PLANE, split_axis=0, concat_axis=0, tiled=True)
    partial = parts.reshape(plane, share, depth).sum(0).astype(jnp.bfloat16)
    partial, used = lax.optimization_barrier((partial, used))
    middle = after_step([used, *lists[1:]], both, block_values)
    copies = jnp.broadcast_to(partial[None], (line, share, depth))
    copies = lax.all_to_all(copies, LINE, split_axis=0, concat_axis=0, tiled=True)
    factor = 1.0 / math.sqrt(rows_part * lax.axis_size(DOM))
    grads = copies.reshape(line, share, depth).astype(jnp.float32).sum(0) * factor
    total = total_step(middle, from_prev, from_next)
    total, grads = lax.optimization_barrier((total, grads.astype(jnp.bfloat16)))
    feature_grad = lax.all_to_all(total, "feat", split_axis=0, concat_axis=1, tiled=True)
    grads = collected(grads)
    return (feature_grad, grads[:depth], grads[depth:])


def solution(mesh):
    fine = Mesh(mesh.devices.reshape(2, 4, 4, 2, 8), RING)
    return jax.shard_map(
        on_device,
        mesh=fine,
        in_specs=(
            P("feat", DOM),
            P(DOM, None),
            P(DOM, None),
            P(DOM),
            P(DOM, None, None),
            P(),
            P(),
            P(None, RING),
        ),
        out_specs=(P("feat", DOM), P(), P()),
        check_vma=False,
    )
```

```python
import functools
import math

import jax
import jax.numpy as jnp
from jax import lax
from jax.experimental import pallas as pl
from jax.experimental.pallas import tpu as pltpu
from jax.sharding import Mesh, PartitionSpec as P

BLK = 128
REACH = 8
DOM = ("zh", "y", "x", "core")
PLANE = ("y", "x", "core")
LINE = ("zh", "feat")
RING = DOM + ("feat",)


def shifted(shard, axis, by):
    count = lax.axis_size(axis)
    return lax.ppermute(shard, axis, [(i, (i + by) % count) for i in range(count)])


def collected(rows):
    for axis in reversed(PLANE):
        count = lax.axis_size(axis)
        apart = 1
        while apart < count:
            other = lax.ppermute(rows, axis, [(i, i ^ apart) for i in range(count)])
            second = (lax.axis_index(axis) & apart) != 0
            rows = jnp.concatenate(
                [jnp.where(second, other, rows), jnp.where(second, rows, other)], axis=0
            )
            apart *= 2
    return rows


def tiles_of(width, tile):
    return [(at, min(tile, width - at)) for at in range(0, width, tile)]


SMEM = pl.BlockSpec(memory_space=pltpu.SMEM)
VMEM = pl.BlockSpec(memory_space=pltpu.VMEM)
HBM = pl.BlockSpec(memory_space=pltpu.HBM)
LEFT, OWN, RIGHT = range(3)


def list_kernel(chunk, rows_ref, cols_ref, count_ref, pos_ref, used_ref, slot_ref, row_ref, col_ref):
    slots = rows_ref.shape[0]
    first = pos_ref[0] * chunk
    for kind in range(3):
        used_ref[kind] = 0

    def step(slot, carry):
        row = rows_ref[slot] - first

        @pl.when((row >= 0) & (row < chunk))
        def _():
            col = cols_ref[slot] - first - REACH
            kind = jnp.where(col < 0, LEFT, jnp.where(col < chunk, OWN, RIGHT))
            base = jnp.where(col < 0, REACH, jnp.where(col < chunk, 0, -chunk))
            at = kind * slots + used_ref[kind]
            slot_ref[at] = slot
            row_ref[at] = row
            col_ref[at] = col + base
            used_ref[kind] = used_ref[kind] + 1

        return carry

    lax.fori_loop(0, jnp.minimum(count_ref[0], slots), step, 0)


def list_step(rows, cols, count, pos, chunk):
    table = jax.ShapeDtypeStruct((3 * rows.shape[0],), jnp.int32)
    return pl.pallas_call(
        functools.partial(list_kernel, chunk),
        out_shape=(jax.ShapeDtypeStruct((3,), jnp.int32), table, table, table),
        in_specs=[SMEM] * 4,
        out_specs=(SMEM,) * 4,
        cost_estimate=pl.CostEstimate(flops=0, bytes_accessed=4096, transcendentals=0),
    )(rows, cols, count, pos)


def block(index):
    return pl.ds(pl.multiple_of(index * BLK, BLK), BLK)


def add_slots(lists, kind, source, into, values, forward):
    used_ref, slot_ref, row_ref, col_ref = lists
    base = kind * (slot_ref.shape[0] // 3)
    count = used_ref[kind]

    def some(indices):
        products = []
        for at in indices:
            read = col_ref[at] if forward else row_ref[at]
            products.append(
                lax.dot_general(
                    source[:, block(read)],
                    values[slot_ref[at]],
                    (((1,), (1 if forward else 0,)), ((), ())),
                    preferred_element_type=jnp.float32,
                )
            )
        for at, product in zip(indices, products):
            write = row_ref[at] if forward else col_ref[at]
            into[:, block(write)] += product

    def pair(step, carry):
        some([base + 2 * step, base + 2 * step + 1])
        return carry

    lax.fori_loop(0, lax.div(count, 2), pair, 0)

    @pl.when(lax.rem(count, 2) == 1)
    def _():
        some([base + count - 1])


def before_kernel(pos_ref, *refs):
    lists, (own_ref, values_ref, prev_ref, next_ref) = refs[:4], refs[4:8]
    piece_refs, (agg_ref, rim_ref) = refs[8:-2], refs[-2:]
    agg_ref[...] = jnp.zeros_like(agg_ref)
    add_slots(lists, OWN, own_ref, agg_ref, values_ref, True)
    last = len(piece_refs)
    height = prev_ref.shape[0]

    @pl.when(pos_ref[0] == 0)
    def _():
        for group, ref in enumerate((prev_ref, *piece_refs)):
            rim_ref[group * height : (group + 1) * height] = ref[...]

    @pl.when(pos_ref[0] != 0)
    def _():
        for group, ref in enumerate((next_ref, *piece_refs)):
            rim_ref[(last - group) * height : (last - group + 1) * height] = ref[...]


def before_step(pos, lists, own, values, prev_part, next_part, gathered):
    depth, rim = own.shape[0], prev_part.shape[1]
    return pl.pallas_call(
        before_kernel,
        out_shape=(
            jax.ShapeDtypeStruct(own.shape, jnp.float32),
            jax.ShapeDtypeStruct((depth, rim), own.dtype),
        ),
        in_specs=[SMEM] * 5 + [VMEM] * (4 + len(gathered)),
        out_specs=(VMEM,) * 2,
        compiler_params=pltpu.CompilerParams(vmem_limit_bytes=24 * 1024 * 1024),
        cost_estimate=pl.CostEstimate(flops=1 << 28, bytes_accessed=4 << 20, transcendentals=0),
    )(pos, *lists, own, values, prev_part, next_part, *gathered)


def local_kernel(last, pos_ref, *refs):
    lists = refs[:4]
    agg_ref, own_ref, before_ref, after_ref, rim_ref, values_ref = refs[4:10]
    w_in_ref, w_out_ref, cot_ref = refs[10:13]
    terms_ref, both_ref, stacked, delta, agg, held, terms, sems = refs[13:]
    depth, width = own_ref.shape
    agg[...] = agg_ref[...]
    for kind, ref, edge in ((LEFT, before_ref, 0), (RIGHT, after_ref, last)):
        pl.when(pos_ref[0] == edge)(
            functools.partial(add_slots, lists, kind, rim_ref, agg, values_ref, True)
        )
        pl.when(pos_ref[0] != edge)(
            functools.partial(add_slots, lists, kind, ref, agg, values_ref, True)
        )
    for at, size in tiles_of(width, 256):
        part = slice(at, at + size)
        stacked[:depth, part] = own_ref[:, part]
        stacked[depth:, part] = agg[:, part].astype(jnp.bfloat16)
        preact = jnp.dot(w_in_ref[...], stacked[:, part], preferred_element_type=jnp.float32)
        sigma = 1.0 / (1.0 + jnp.exp(-preact))
        slope = sigma * (1.0 + preact * (1.0 - sigma))
        delta[:, part] = (cot_ref[:, part].astype(jnp.float32) * slope).astype(jnp.bfloat16)
        both = jnp.dot(w_out_ref[...], delta[:, part], preferred_element_type=jnp.float32)
        held[:, part] = both.astype(jnp.bfloat16)
    first = pltpu.make_async_copy(held, both_ref, sems.at[0])
    first.start()
    terms[...] = lax.dot_general(
        stacked[...], delta[...], (((1,), (1,)), ((), ())), preferred_element_type=jnp.float32
    )
    second = pltpu.make_async_copy(terms, terms_ref, sems.at[1])
    second.start()
    first.wait()
    second.wait()


def edge_kernel(*refs):
    lists, (both_ref, values_ref, left_ref, right_ref, agg_grad, scat, sem) = refs[:4], refs[4:]
    depth = left_ref.shape[0]
    fetch = pltpu.make_async_copy(both_ref.at[pl.ds(depth, depth)], agg_grad, sem)
    fetch.start()
    fetch.wait()
    for kind, out_ref in ((LEFT, left_ref), (RIGHT, right_ref)):
        scat[...] = jnp.zeros_like(scat)
        add_slots(lists, kind, agg_grad, scat, values_ref, False)
        out_ref[...] = scat[...].astype(jnp.bfloat16)


def edge_step(lists, both, values, rim):
    depth, width = both.shape[0] // 2, both.shape[1]
    return pl.pallas_call(
        edge_kernel,
        out_shape=(jax.ShapeDtypeStruct((depth, rim), jnp.bfloat16),) * 2,
        in_specs=[SMEM] * 4 + [HBM, VMEM],
        out_specs=(VMEM,) * 2,
        scratch_shapes=[
            pltpu.VMEM((depth, width), jnp.bfloat16),
            pltpu.VMEM((depth, rim), jnp.float32),
            pltpu.SemaphoreType.DMA,
        ],
        compiler_params=pltpu.CompilerParams(vmem_limit_bytes=24 * 1024 * 1024),
        cost_estimate=pl.CostEstimate(flops=1 << 28, bytes_accessed=4 << 20, transcendentals=0),
    )(*lists, both, values)


def local_step(pos, lists, agg, own, before, after, rim_part, values, w_in, w_out, cot):
    depth, width = own.shape
    both = jax.ShapeDtypeStruct((2 * depth, width), jnp.bfloat16)
    return pl.pallas_call(
        functools.partial(local_kernel, lax.axis_size("feat") - 1),
        out_shape=(jax.ShapeDtypeStruct((2 * depth, depth), jnp.float32), both),
        in_specs=[SMEM] * 5 + [VMEM] * 9,
        out_specs=(HBM, HBM),
        scratch_shapes=[
            pltpu.VMEM((2 * depth, width), jnp.bfloat16),
            pltpu.VMEM((depth, width), jnp.bfloat16),
            pltpu.VMEM((depth, width), jnp.float32),
            pltpu.VMEM((2 * depth, width), jnp.bfloat16),
            pltpu.VMEM((2 * depth, depth), jnp.float32),
            pltpu.SemaphoreType.DMA((2,)),
        ],
        compiler_params=pltpu.CompilerParams(vmem_limit_bytes=40 * 1024 * 1024),
        cost_estimate=pl.CostEstimate(
            flops=12 * depth * depth * width, bytes_accessed=8 << 20, transcendentals=depth * width
        ),
    )(pos, *lists, agg, own, before, after, rim_part, values, w_in, w_out, cot)


def after_kernel(*refs):
    lists, (both_ref, values_ref, middle_ref) = refs[:4], refs[4:]
    depth = middle_ref.shape[0]
    middle_ref[...] = both_ref[:depth].astype(jnp.float32)
    add_slots(lists, OWN, both_ref.at[pl.ds(depth, depth)], middle_ref, values_ref, False)


def after_step(lists, both, values):
    return pl.pallas_call(
        after_kernel,
        out_shape=jax.ShapeDtypeStruct((both.shape[0] // 2, both.shape[1]), jnp.float32),
        in_specs=[SMEM] * 4 + [VMEM] * 2,
        out_specs=VMEM,
        compiler_params=pltpu.CompilerParams(vmem_limit_bytes=24 * 1024 * 1024),
        cost_estimate=pl.CostEstimate(flops=1 << 28, bytes_accessed=6 << 20, transcendentals=0),
    )(*lists, both, values)


def total_kernel(middle_ref, prev_ref, next_ref, out_ref):
    width, rim = middle_ref.shape[1], prev_ref.shape[1]
    edges = sorted({0, min(rim, width - rim), max(rim, width - rim), width})
    for at, end in zip(edges, edges[1:]):
        part = middle_ref[:, at:end]
        if at < rim:
            part = part + prev_ref[:, at:end].astype(jnp.float32)
        if at >= width - rim:
            here = at - (width - rim)
            part = part + next_ref[:, here : here + end - at].astype(jnp.float32)
        out_ref[:, at:end] = part.astype(jnp.bfloat16)


def total_step(middle, from_prev, from_next):
    return pl.pallas_call(
        total_kernel,
        out_shape=jax.ShapeDtypeStruct(middle.shape, jnp.bfloat16),
        in_specs=[VMEM] * 3,
        out_specs=VMEM,
        compiler_params=pltpu.CompilerParams(vmem_limit_bytes=24 * 1024 * 1024),
        cost_estimate=pl.CostEstimate(flops=0, bytes_accessed=4 << 20, transcendentals=0),
    )(middle, from_prev, from_next)


def cut_kernel(pos_ref, features_ref, *refs):
    piece_refs, sems = refs[:-1], refs[-1]
    pieces, width = len(piece_refs), piece_refs[0].shape[1]
    copies = []
    for step, piece_ref in enumerate(piece_refs):
        dest = lax.rem(pos_ref[0] + step, pieces)
        part = pl.ds(pl.multiple_of(dest * width, BLK), width)
        copies.append(pltpu.make_async_copy(features_ref.at[:, part], piece_ref, sems.at[step]))
    for copy in copies:
        copy.start()
    for copy in copies:
        copy.wait()


def cut_step(pos, features, pieces):
    height, width = features.shape[0], features.shape[1] // pieces
    return pl.pallas_call(
        cut_kernel,
        out_shape=(jax.ShapeDtypeStruct((height, width), features.dtype),) * pieces,
        in_specs=[SMEM, pl.BlockSpec(memory_space=pl.ANY)],
        out_specs=(VMEM,) * pieces,
        scratch_shapes=[pltpu.SemaphoreType.DMA((pieces,))],
        compiler_params=pltpu.CompilerParams(vmem_limit_bytes=16 * 1024 * 1024),
        cost_estimate=pl.CostEstimate(flops=0, bytes_accessed=2 << 20, transcendentals=0),
    )(pos, features)


def join_kernel(pos_ref, *refs):
    piece_refs, (own_ref, head_ref, tail_ref) = refs[:-3], refs[-3:]
    pieces = len(piece_refs)
    height, width = piece_refs[0].shape
    rim = head_ref.shape[1]
    for step, piece_ref in enumerate(piece_refs):
        source = lax.rem(pos_ref[0] + pieces - step, pieces)
        rows = pl.ds(pl.multiple_of(source * height, height), height)
        own_ref[rows, :] = piece_ref[...]
        head_ref[rows, :] = piece_ref[:, :rim]
        tail_ref[rows, :] = piece_ref[:, width - rim :]


def join_step(pos, received, rim):
    pieces = len(received)
    height, width = received[0].shape
    depth, kind = pieces * height, received[0].dtype
    edge = jax.ShapeDtypeStruct((depth, rim), kind)
    return pl.pallas_call(
        join_kernel,
        out_shape=(jax.ShapeDtypeStruct((depth, width), kind), edge, edge),
        in_specs=[SMEM] + [VMEM] * pieces,
        out_specs=(VMEM,) * 3,
        compiler_params=pltpu.CompilerParams(vmem_limit_bytes=16 * 1024 * 1024),
        cost_estimate=pl.CostEstimate(flops=0, bytes_accessed=4 << 20, transcendentals=0),
    )(pos, *received)


def on_device(
    features, block_row, block_col, block_count, block_values, w_self, w_neigh, cotangent
):
    rows_part = features.shape[1]
    depth, width = cotangent.shape
    rim = REACH * BLK
    chunk = width // BLK
    pos = lax.axis_index("feat").astype(jnp.int32)[None]
    lists = list_step(block_row[0], block_col[0], block_count, pos, chunk)
    w_in = jnp.concatenate([w_self.T, w_neigh.T], axis=1)
    w_out = jnp.concatenate([w_self, w_neigh], axis=0)
    pieces = lax.axis_size("feat")
    received = list(cut_step(pos, features, pieces))
    for step in sorted(range(1, pieces), key=lambda step: (abs(2 * step - pieces), step)):
        received[step] = shifted(received[step], "feat", step)
    prev_part = shifted(features[:, rows_part - rim :], DOM, 1)
    next_part = shifted(features[:, :rim], DOM, -1)
    gathered = []
    for step in range(1, pieces):
        part = jnp.where(pos[0] == step, prev_part, next_part)
        gathered.append(
            lax.ppermute(part, "feat", [(step, 0), (pieces - 1 - step, pieces - 1)])
        )
    *received, gathered = lax.optimization_barrier((*received, gathered))
    own, head, tail = join_step(pos, received, rim)
    before = lax.ppermute(tail, "feat", [(i, i + 1) for i in range(pieces - 1)])
    after = lax.ppermute(head, "feat", [(i + 1, i) for i in range(pieces - 1)])
    agg, rim_part = before_step(pos, lists, own, block_values, prev_part, next_part, gathered)
    terms, both = local_step(
        pos, lists, agg, own, before, after, rim_part, block_values, w_in, w_out, cotangent
    )
    plane, line = lax.axis_size(PLANE), lax.axis_size(LINE)
    share = 2 * depth // plane
    used, terms = lax.optimization_barrier((lists[0], terms))
    left, right = edge_step([used, *lists[1:]], both, block_values, rim)
    from_next = shifted(left, RING, -1)
    from_prev = shifted(right, RING, 1)
    parts = lax.all_to_all(terms, PLANE, split_axis=0, concat_axis=0, tiled=True)
    partial = parts.reshape(plane, share, depth).sum(0).astype(jnp.bfloat16)
    partial, used = lax.optimization_barrier((partial, used))
    middle = after_step([used, *lists[1:]], both, block_values)
    copies = jnp.broadcast_to(partial[None], (line, share, depth))
    copies = lax.all_to_all(copies, LINE, split_axis=0, concat_axis=0, tiled=True)
    factor = 1.0 / math.sqrt(rows_part * lax.axis_size(DOM))
    grads = copies.reshape(line, share, depth).astype(jnp.float32).sum(0) * factor
    total = total_step(middle, from_prev, from_next)
    total, grads = lax.optimization_barrier((total, grads.astype(jnp.bfloat16)))
    feature_grad = lax.all_to_all(total, "feat", split_axis=0, concat_axis=1, tiled=True)
    grads = collected(grads)
    return (feature_grad, grads[:depth], grads[depth:])


def solution(mesh):
    fine = Mesh(mesh.devices.reshape(2, 4, 4, 2, 8), RING)
    return jax.shard_map(
        on_device,
        mesh=fine,
        in_specs=(
            P("feat", DOM),
            P(DOM, None),
            P(DOM, None),
            P(DOM),
            P(DOM, None, None),
            P(),
            P(),
            P(None, RING),
        ),
        out_specs=(P("feat", DOM), P(), P()),
        check_vma=False,
    )
```

```python
import functools
import math

import jax
import jax.numpy as jnp
from jax import lax
from jax.experimental import pallas as pl
from jax.experimental.pallas import tpu as pltpu
from jax.sharding import Mesh, PartitionSpec as P

BLK = 128
REACH = 8
DOM = ("zh", "y", "x", "core")
PLANE = ("y", "x", "core")
LINE = ("zh", "feat")
RING = DOM + ("feat",)


def shifted(shard, axis, by):
    count = lax.axis_size(axis)
    return lax.ppermute(shard, axis, [(i, (i + by) % count) for i in range(count)])


def collected(rows):
    for axis in reversed(PLANE):
        count = lax.axis_size(axis)
        apart = 1
        while apart < count:
            other = lax.ppermute(rows, axis, [(i, i ^ apart) for i in range(count)])
            second = (lax.axis_index(axis) & apart) != 0
            rows = jnp.concatenate(
                [jnp.where(second, other, rows), jnp.where(second, rows, other)], axis=0
            )
            apart *= 2
    return rows


def tiles_of(width, tile):
    return [(at, min(tile, width - at)) for at in range(0, width, tile)]


SMEM = pl.BlockSpec(memory_space=pltpu.SMEM)
VMEM = pl.BlockSpec(memory_space=pltpu.VMEM)
LEFT, OWN, RIGHT = range(3)


def list_kernel(chunk, rows_ref, cols_ref, count_ref, pos_ref, used_ref, slot_ref, row_ref, col_ref):
    slots = rows_ref.shape[0]
    first = pos_ref[0] * chunk
    for kind in range(3):
        used_ref[kind] = 0

    def step(slot, carry):
        row = rows_ref[slot] - first

        @pl.when((row >= 0) & (row < chunk))
        def _():
            col = cols_ref[slot] - first - REACH
            kind = jnp.where(col < 0, LEFT, jnp.where(col < chunk, OWN, RIGHT))
            base = jnp.where(col < 0, REACH, jnp.where(col < chunk, 0, -chunk))
            at = kind * slots + used_ref[kind]
            slot_ref[at] = slot
            row_ref[at] = row
            col_ref[at] = col + base
            used_ref[kind] = used_ref[kind] + 1

        return carry

    lax.fori_loop(0, jnp.minimum(count_ref[0], slots), step, 0)


def list_step(rows, cols, count, pos, chunk):
    table = jax.ShapeDtypeStruct((3 * rows.shape[0],), jnp.int32)
    return pl.pallas_call(
        functools.partial(list_kernel, chunk),
        out_shape=(jax.ShapeDtypeStruct((3,), jnp.int32), table, table, table),
        in_specs=[SMEM] * 4,
        out_specs=(SMEM,) * 4,
        cost_estimate=pl.CostEstimate(flops=0, bytes_accessed=4096, transcendentals=0),
    )(rows, cols, count, pos)


def block(index):
    return pl.ds(pl.multiple_of(index * BLK, BLK), BLK)


def add_slots(lists, kind, source, into, values, forward):
    used_ref, slot_ref, row_ref, col_ref = lists
    base = kind * (slot_ref.shape[0] // 3)
    count = used_ref[kind]

    def some(indices):
        products = []
        for at in indices:
            read = col_ref[at] if forward else row_ref[at]
            products.append(
                lax.dot_general(
                    source[:, block(read)],
                    values[slot_ref[at]],
                    (((1,), (1 if forward else 0,)), ((), ())),
                    preferred_element_type=jnp.float32,
                )
            )
        for at, product in zip(indices, products):
            write = row_ref[at] if forward else col_ref[at]
            into[:, block(write)] += product

    def pair(step, carry):
        some([base + 2 * step, base + 2 * step + 1])
        return carry

    lax.fori_loop(0, lax.div(count, 2), pair, 0)

    @pl.when(lax.rem(count, 2) == 1)
    def _():
        some([base + count - 1])


def before_kernel(*refs):
    lists, (own_ref, values_ref, agg_ref) = refs[:4], refs[4:]
    agg_ref[...] = jnp.zeros_like(agg_ref)
    add_slots(lists, OWN, own_ref, agg_ref, values_ref, True)


def before_step(lists, own, values):
    return pl.pallas_call(
        before_kernel,
        out_shape=jax.ShapeDtypeStruct(own.shape, jnp.float32),
        in_specs=[SMEM] * 4 + [VMEM] * 2,
        out_specs=VMEM,
        compiler_params=pltpu.CompilerParams(vmem_limit_bytes=24 * 1024 * 1024),
        cost_estimate=pl.CostEstimate(flops=1 << 28, bytes_accessed=4 << 20, transcendentals=0),
    )(*lists, own, values)


def local_kernel(*refs):
    lists = refs[:4]
    (agg_ref, own_ref, before_ref, after_ref, values_ref, w_in_ref, w_out_ref, cot_ref) = refs[4:12]
    left_ref, right_ref, terms_ref, both_ref, stacked, delta, agg, scat = refs[12:]
    depth, width = own_ref.shape
    agg[...] = agg_ref[...]
    add_slots(lists, LEFT, before_ref, agg, values_ref, True)
    add_slots(lists, RIGHT, after_ref, agg, values_ref, True)
    for at, size in tiles_of(width, 256):
        part = slice(at, at + size)
        stacked[:depth, part] = own_ref[:, part]
        stacked[depth:, part] = agg[:, part].astype(jnp.bfloat16)
        preact = jnp.dot(w_in_ref[...], stacked[:, part], preferred_element_type=jnp.float32)
        sigma = 1.0 / (1.0 + jnp.exp(-preact))
        slope = sigma * (1.0 + preact * (1.0 - sigma))
        delta[:, part] = (cot_ref[:, part].astype(jnp.float32) * slope).astype(jnp.bfloat16)
        both = jnp.dot(w_out_ref[...], delta[:, part], preferred_element_type=jnp.float32)
        both_ref[:, part] = both.astype(jnp.bfloat16)
    agg_grad = both_ref.at[pl.ds(depth, depth)]
    for kind, out_ref in ((LEFT, left_ref), (RIGHT, right_ref)):
        scat[...] = jnp.zeros_like(scat)
        add_slots(lists, kind, agg_grad, scat, values_ref, False)
        out_ref[...] = scat[...].astype(jnp.bfloat16)
    terms_ref[...] = lax.dot_general(
        stacked[...], delta[...], (((1,), (1,)), ((), ())), preferred_element_type=jnp.float32
    )


def local_step(lists, agg, own, before, after, values, w_in, w_out, cot):
    depth, width = own.shape
    rim = before.shape[1]
    return pl.pallas_call(
        local_kernel,
        out_shape=(
            jax.ShapeDtypeStruct((depth, rim), jnp.bfloat16),
            jax.ShapeDtypeStruct((depth, rim), jnp.bfloat16),
            jax.ShapeDtypeStruct((2 * depth, depth), jnp.float32),
            jax.ShapeDtypeStruct((2 * depth, width), jnp.bfloat16),
        ),
        in_specs=[SMEM] * 4 + [VMEM] * 8,
        out_specs=(VMEM,) * 4,
        scratch_shapes=[
            pltpu.VMEM((2 * depth, width), jnp.bfloat16),
            pltpu.VMEM((depth, width), jnp.bfloat16),
            pltpu.VMEM((depth, width), jnp.float32),
            pltpu.VMEM((depth, rim), jnp.float32),
        ],
        compiler_params=pltpu.CompilerParams(vmem_limit_bytes=40 * 1024 * 1024),
        cost_estimate=pl.CostEstimate(
            flops=12 * depth * depth * width, bytes_accessed=8 << 20, transcendentals=depth * width
        ),
    )(*lists, agg, own, before, after, values, w_in, w_out, cot)


def after_kernel(*refs):
    lists, (both_ref, values_ref, middle_ref) = refs[:4], refs[4:]
    depth = middle_ref.shape[0]
    middle_ref[...] = both_ref[:depth].astype(jnp.float32)
    add_slots(lists, OWN, both_ref.at[pl.ds(depth, depth)], middle_ref, values_ref, False)


def after_step(lists, both, values):
    return pl.pallas_call(
        after_kernel,
        out_shape=jax.ShapeDtypeStruct((both.shape[0] // 2, both.shape[1]), jnp.float32),
        in_specs=[SMEM] * 4 + [VMEM] * 2,
        out_specs=VMEM,
        compiler_params=pltpu.CompilerParams(vmem_limit_bytes=24 * 1024 * 1024),
        cost_estimate=pl.CostEstimate(flops=1 << 28, bytes_accessed=6 << 20, transcendentals=0),
    )(*lists, both, values)


def total_kernel(middle_ref, prev_ref, next_ref, out_ref):
    width, rim = middle_ref.shape[1], prev_ref.shape[1]
    edges = sorted({0, min(rim, width - rim), max(rim, width - rim), width})
    for at, end in zip(edges, edges[1:]):
        part = middle_ref[:, at:end]
        if at < rim:
            part = part + prev_ref[:, at:end].astype(jnp.float32)
        if at >= width - rim:
            here = at - (width - rim)
            part = part + next_ref[:, here : here + end - at].astype(jnp.float32)
        out_ref[:, at:end] = part.astype(jnp.bfloat16)


def total_step(middle, from_prev, from_next):
    return pl.pallas_call(
        total_kernel,
        out_shape=jax.ShapeDtypeStruct(middle.shape, jnp.bfloat16),
        in_specs=[VMEM] * 3,
        out_specs=VMEM,
        compiler_params=pltpu.CompilerParams(vmem_limit_bytes=24 * 1024 * 1024),
        cost_estimate=pl.CostEstimate(flops=0, bytes_accessed=4 << 20, transcendentals=0),
    )(middle, from_prev, from_next)


def cut_kernel(pos_ref, features_ref, *refs):
    piece_refs, sems = refs[:-1], refs[-1]
    pieces, width = len(piece_refs), piece_refs[0].shape[1]
    copies = []
    for step, piece_ref in enumerate(piece_refs):
        dest = lax.rem(pos_ref[0] + step, pieces)
        part = pl.ds(pl.multiple_of(dest * width, BLK), width)
        copies.append(pltpu.make_async_copy(features_ref.at[:, part], piece_ref, sems.at[step]))
    for copy in copies:
        copy.start()
    for copy in copies:
        copy.wait()


def cut_step(pos, features, pieces):
    height, width = features.shape[0], features.shape[1] // pieces
    return pl.pallas_call(
        cut_kernel,
        out_shape=(jax.ShapeDtypeStruct((height, width), features.dtype),) * pieces,
        in_specs=[SMEM, pl.BlockSpec(memory_space=pl.ANY)],
        out_specs=(VMEM,) * pieces,
        scratch_shapes=[pltpu.SemaphoreType.DMA((pieces,))],
        compiler_params=pltpu.CompilerParams(vmem_limit_bytes=16 * 1024 * 1024),
        cost_estimate=pl.CostEstimate(flops=0, bytes_accessed=2 << 20, transcendentals=0),
    )(pos, features)


def join_kernel(pos_ref, *refs):
    piece_refs, (own_ref, head_ref, tail_ref) = refs[:-3], refs[-3:]
    pieces = len(piece_refs)
    height, width = piece_refs[0].shape
    rim = head_ref.shape[1]
    for step, piece_ref in enumerate(piece_refs):
        source = lax.rem(pos_ref[0] + pieces - step, pieces)
        rows = pl.ds(pl.multiple_of(source * height, height), height)
        own_ref[rows, :] = piece_ref[...]
        head_ref[rows, :] = piece_ref[:, :rim]
        tail_ref[rows, :] = piece_ref[:, width - rim :]


def join_step(pos, received, rim):
    pieces = len(received)
    height, width = received[0].shape
    depth, kind = pieces * height, received[0].dtype
    edge = jax.ShapeDtypeStruct((depth, rim), kind)
    return pl.pallas_call(
        join_kernel,
        out_shape=(jax.ShapeDtypeStruct((depth, width), kind), edge, edge),
        in_specs=[SMEM] + [VMEM] * pieces,
        out_specs=(VMEM,) * 3,
        compiler_params=pltpu.CompilerParams(vmem_limit_bytes=16 * 1024 * 1024),
        cost_estimate=pl.CostEstimate(flops=0, bytes_accessed=4 << 20, transcendentals=0),
    )(pos, *received)


def on_device(
    features, block_row, block_col, block_count, block_values, w_self, w_neigh, cotangent
):
    rows_part = features.shape[1]
    depth, width = cotangent.shape
    rim = REACH * BLK
    chunk = width // BLK
    pos = lax.axis_index("feat").astype(jnp.int32)[None]
    lists = list_step(block_row[0], block_col[0], block_count, pos, chunk)
    w_in = jnp.concatenate([w_self.T, w_neigh.T], axis=1)
    w_out = jnp.concatenate([w_self, w_neigh], axis=0)
    pieces = lax.axis_size("feat")
    received = list(cut_step(pos, features, pieces))
    for step in sorted(range(1, pieces), key=lambda step: (abs(2 * step - pieces), step)):
        received[step] = shifted(received[step], "feat", step)
    own, head, tail = join_step(pos, received, rim)
    before = shifted(tail, RING, 1)
    after = shifted(head, RING, -1)
    agg = before_step(lists, own, block_values)
    left, right, terms, both = local_step(
        lists, agg, own, before, after, block_values, w_in, w_out, cotangent
    )
    plane, line = lax.axis_size(PLANE), lax.axis_size(LINE)
    share = 2 * depth // plane
    from_next = shifted(left, RING, -1)
    from_prev = shifted(right, RING, 1)
    parts = lax.all_to_all(terms, PLANE, split_axis=0, concat_axis=0, tiled=True)
    partial = parts.reshape(plane, share, depth).sum(0).astype(jnp.bfloat16)
    middle = after_step(lists, both, block_values)
    partial, from_next, from_prev, middle = lax.optimization_barrier(
        (partial, from_next, from_prev, middle)
    )
    copies = jnp.broadcast_to(partial[None], (line, share, depth))
    copies = lax.all_to_all(copies, LINE, split_axis=0, concat_axis=0, tiled=True)
    factor = 1.0 / math.sqrt(rows_part * lax.axis_size(DOM))
    grads = copies.reshape(line, share, depth).astype(jnp.float32).sum(0) * factor
    total = total_step(middle, from_prev, from_next)
    total, grads = lax.optimization_barrier((total, grads.astype(jnp.bfloat16)))
    feature_grad = lax.all_to_all(total, "feat", split_axis=0, concat_axis=1, tiled=True)
    grads = collected(grads)
    return (feature_grad, grads[:depth], grads[depth:])


def solution(mesh):
    fine = Mesh(mesh.devices.reshape(2, 4, 4, 2, 8), RING)
    return jax.shard_map(
        on_device,
        mesh=fine,
        in_specs=(
            P("feat", DOM),
            P(DOM, None),
            P(DOM, None),
            P(DOM),
            P(DOM, None, None),
            P(),
            P(),
            P(None, RING),
        ),
        out_specs=(P("feat", DOM), P(), P()),
        check_vma=False,
    )
```

```python
import functools
import math

import jax
import jax.numpy as jnp
from jax import lax
from jax.experimental import pallas as pl
from jax.experimental.pallas import tpu as pltpu
from jax.sharding import Mesh, PartitionSpec as P

BLK = 128
REACH = 8
DOM = ("zh", "y", "x", "core")
PLANE = ("y", "x", "core")
LINE = ("zh", "feat")
RING = DOM + ("feat",)


def shifted(shard, axis, by):
    count = lax.axis_size(axis)
    return lax.ppermute(shard, axis, [(i, (i + by) % count) for i in range(count)])


def collected(rows):
    for axis in reversed(PLANE):
        count = lax.axis_size(axis)
        apart = 1
        while apart < count:
            other = lax.ppermute(rows, axis, [(i, i ^ apart) for i in range(count)])
            second = (lax.axis_index(axis) & apart) != 0
            rows = jnp.concatenate(
                [jnp.where(second, other, rows), jnp.where(second, rows, other)], axis=0
            )
            apart *= 2
    return rows


def tiles_of(width, tile):
    return [(at, min(tile, width - at)) for at in range(0, width, tile)]


SMEM = pl.BlockSpec(memory_space=pltpu.SMEM)
VMEM = pl.BlockSpec(memory_space=pltpu.VMEM)
LEFT, OWN, RIGHT = range(3)


def list_kernel(chunk, rows_ref, cols_ref, count_ref, pos_ref, used_ref, slot_ref, row_ref, col_ref):
    slots = rows_ref.shape[0]
    first = pos_ref[0] * chunk
    for kind in range(3):
        used_ref[kind] = 0

    def step(slot, carry):
        row = rows_ref[slot] - first

        @pl.when((row >= 0) & (row < chunk))
        def _():
            col = cols_ref[slot] - first - REACH
            kind = jnp.where(col < 0, LEFT, jnp.where(col < chunk, OWN, RIGHT))
            base = jnp.where(col < 0, REACH, jnp.where(col < chunk, 0, -chunk))
            at = kind * slots + used_ref[kind]
            slot_ref[at] = slot
            row_ref[at] = row
            col_ref[at] = col + base
            used_ref[kind] = used_ref[kind] + 1

        return carry

    lax.fori_loop(0, jnp.minimum(count_ref[0], slots), step, 0)


def list_step(rows, cols, count, pos, chunk):
    table = jax.ShapeDtypeStruct((3 * rows.shape[0],), jnp.int32)
    return pl.pallas_call(
        functools.partial(list_kernel, chunk),
        out_shape=(jax.ShapeDtypeStruct((3,), jnp.int32), table, table, table),
        in_specs=[SMEM] * 4,
        out_specs=(SMEM,) * 4,
        cost_estimate=pl.CostEstimate(flops=0, bytes_accessed=4096, transcendentals=0),
    )(rows, cols, count, pos)


def block(index):
    return pl.ds(pl.multiple_of(index * BLK, BLK), BLK)


def add_slots(lists, kind, source, into, values, forward):
    used_ref, slot_ref, row_ref, col_ref = lists
    base = kind * (slot_ref.shape[0] // 3)
    count = used_ref[kind]

    def some(indices):
        products = []
        for at in indices:
            read = col_ref[at] if forward else row_ref[at]
            products.append(
                lax.dot_general(
                    source[:, block(read)],
                    values[slot_ref[at]],
                    (((1,), (1 if forward else 0,)), ((), ())),
                    preferred_element_type=jnp.float32,
                )
            )
        for at, product in zip(indices, products):
            write = row_ref[at] if forward else col_ref[at]
            into[:, block(write)] += product

    def pair(step, carry):
        some([base + 2 * step, base + 2 * step + 1])
        return carry

    lax.fori_loop(0, lax.div(count, 2), pair, 0)

    @pl.when(lax.rem(count, 2) == 1)
    def _():
        some([base + count - 1])


def before_kernel(*refs):
    lists, (own_ref, values_ref, agg_ref) = refs[:4], refs[4:]
    agg_ref[...] = jnp.zeros_like(agg_ref)
    add_slots(lists, OWN, own_ref, agg_ref, values_ref, True)


def before_step(lists, own, values):
    return pl.pallas_call(
        before_kernel,
        out_shape=jax.ShapeDtypeStruct(own.shape, jnp.float32),
        in_specs=[SMEM] * 4 + [VMEM] * 2,
        out_specs=VMEM,
        compiler_params=pltpu.CompilerParams(vmem_limit_bytes=24 * 1024 * 1024),
        cost_estimate=pl.CostEstimate(flops=1 << 28, bytes_accessed=4 << 20, transcendentals=0),
    )(*lists, own, values)


def local_kernel(*refs):
    lists = refs[:4]
    (agg_ref, own_ref, before_ref, after_ref, values_ref, w_in_ref, w_out_ref, cot_ref) = refs[4:12]
    left_ref, right_ref, terms_ref, both_ref, stacked, delta, agg, scat = refs[12:]
    depth, width = own_ref.shape
    agg[...] = agg_ref[...]
    add_slots(lists, LEFT, before_ref, agg, values_ref, True)
    add_slots(lists, RIGHT, after_ref, agg, values_ref, True)
    for at, size in tiles_of(width, 256):
        part = slice(at, at + size)
        stacked[:depth, part] = own_ref[:, part]
        stacked[depth:, part] = agg[:, part].astype(jnp.bfloat16)
        preact = jnp.dot(w_in_ref[...], stacked[:, part], preferred_element_type=jnp.float32)
        sigma = 1.0 / (1.0 + jnp.exp(-preact))
        slope = sigma * (1.0 + preact * (1.0 - sigma))
        delta[:, part] = (cot_ref[:, part].astype(jnp.float32) * slope).astype(jnp.bfloat16)
        both = jnp.dot(w_out_ref[...], delta[:, part], preferred_element_type=jnp.float32)
        both_ref[:, part] = both.astype(jnp.bfloat16)
    agg_grad = both_ref.at[pl.ds(depth, depth)]
    for kind, out_ref in ((LEFT, left_ref), (RIGHT, right_ref)):
        scat[...] = jnp.zeros_like(scat)
        add_slots(lists, kind, agg_grad, scat, values_ref, False)
        out_ref[...] = scat[...].astype(jnp.bfloat16)
    terms_ref[...] = lax.dot_general(
        stacked[...], delta[...], (((1,), (1,)), ((), ())), preferred_element_type=jnp.float32
    )


def local_step(lists, agg, own, before, after, values, w_in, w_out, cot):
    depth, width = own.shape
    rim = before.shape[1]
    return pl.pallas_call(
        local_kernel,
        out_shape=(
            jax.ShapeDtypeStruct((depth, rim), jnp.bfloat16),
            jax.ShapeDtypeStruct((depth, rim), jnp.bfloat16),
            jax.ShapeDtypeStruct((2 * depth, depth), jnp.float32),
            jax.ShapeDtypeStruct((2 * depth, width), jnp.bfloat16),
        ),
        in_specs=[SMEM] * 4 + [VMEM] * 8,
        out_specs=(VMEM,) * 4,
        scratch_shapes=[
            pltpu.VMEM((2 * depth, width), jnp.bfloat16),
            pltpu.VMEM((depth, width), jnp.bfloat16),
            pltpu.VMEM((depth, width), jnp.float32),
            pltpu.VMEM((depth, rim), jnp.float32),
        ],
        compiler_params=pltpu.CompilerParams(vmem_limit_bytes=40 * 1024 * 1024),
        cost_estimate=pl.CostEstimate(
            flops=12 * depth * depth * width, bytes_accessed=8 << 20, transcendentals=depth * width
        ),
    )(*lists, agg, own, before, after, values, w_in, w_out, cot)


def after_kernel(*refs):
    lists, (both_ref, values_ref, middle_ref) = refs[:4], refs[4:]
    depth = middle_ref.shape[0]
    middle_ref[...] = both_ref[:depth].astype(jnp.float32)
    add_slots(lists, OWN, both_ref.at[pl.ds(depth, depth)], middle_ref, values_ref, False)


def after_step(lists, both, values):
    return pl.pallas_call(
        after_kernel,
        out_shape=jax.ShapeDtypeStruct((both.shape[0] // 2, both.shape[1]), jnp.float32),
        in_specs=[SMEM] * 4 + [VMEM] * 2,
        out_specs=VMEM,
        compiler_params=pltpu.CompilerParams(vmem_limit_bytes=24 * 1024 * 1024),
        cost_estimate=pl.CostEstimate(flops=1 << 28, bytes_accessed=6 << 20, transcendentals=0),
    )(*lists, both, values)


def total_kernel(middle_ref, prev_ref, next_ref, out_ref):
    width, rim = middle_ref.shape[1], prev_ref.shape[1]
    edges = sorted({0, min(rim, width - rim), max(rim, width - rim), width})
    for at, end in zip(edges, edges[1:]):
        part = middle_ref[:, at:end]
        if at < rim:
            part = part + prev_ref[:, at:end].astype(jnp.float32)
        if at >= width - rim:
            here = at - (width - rim)
            part = part + next_ref[:, here : here + end - at].astype(jnp.float32)
        out_ref[:, at:end] = part.astype(jnp.bfloat16)


def total_step(middle, from_prev, from_next):
    return pl.pallas_call(
        total_kernel,
        out_shape=jax.ShapeDtypeStruct(middle.shape, jnp.bfloat16),
        in_specs=[VMEM] * 3,
        out_specs=VMEM,
        compiler_params=pltpu.CompilerParams(vmem_limit_bytes=24 * 1024 * 1024),
        cost_estimate=pl.CostEstimate(flops=0, bytes_accessed=4 << 20, transcendentals=0),
    )(middle, from_prev, from_next)


def cut_kernel(pos_ref, features_ref, *refs):
    piece_refs, sems = refs[:-1], refs[-1]
    pieces, width = len(piece_refs), piece_refs[0].shape[1]
    copies = []
    for step, piece_ref in enumerate(piece_refs):
        dest = lax.rem(pos_ref[0] + step, pieces)
        part = pl.ds(pl.multiple_of(dest * width, BLK), width)
        copies.append(pltpu.make_async_copy(features_ref.at[:, part], piece_ref, sems.at[step]))
    for copy in copies:
        copy.start()
    for copy in copies:
        copy.wait()


def cut_step(pos, features, pieces):
    height, width = features.shape[0], features.shape[1] // pieces
    return pl.pallas_call(
        cut_kernel,
        out_shape=(jax.ShapeDtypeStruct((height, width), features.dtype),) * pieces,
        in_specs=[SMEM, pl.BlockSpec(memory_space=pl.ANY)],
        out_specs=(VMEM,) * pieces,
        scratch_shapes=[pltpu.SemaphoreType.DMA((pieces,))],
        compiler_params=pltpu.CompilerParams(vmem_limit_bytes=16 * 1024 * 1024),
        cost_estimate=pl.CostEstimate(flops=0, bytes_accessed=2 << 20, transcendentals=0),
    )(pos, features)


def join_kernel(pos_ref, *refs):
    piece_refs, (own_ref, head_ref, tail_ref) = refs[:-3], refs[-3:]
    pieces = len(piece_refs)
    height, width = piece_refs[0].shape
    rim = head_ref.shape[1]
    for step, piece_ref in enumerate(piece_refs):
        source = lax.rem(pos_ref[0] + pieces - step, pieces)
        rows = pl.ds(pl.multiple_of(source * height, height), height)
        own_ref[rows, :] = piece_ref[...]
        head_ref[rows, :] = piece_ref[:, :rim]
        tail_ref[rows, :] = piece_ref[:, width - rim :]


def join_step(pos, received, rim):
    pieces = len(received)
    height, width = received[0].shape
    depth, kind = pieces * height, received[0].dtype
    edge = jax.ShapeDtypeStruct((depth, rim), kind)
    return pl.pallas_call(
        join_kernel,
        out_shape=(jax.ShapeDtypeStruct((depth, width), kind), edge, edge),
        in_specs=[SMEM] + [VMEM] * pieces,
        out_specs=(VMEM,) * 3,
        compiler_params=pltpu.CompilerParams(vmem_limit_bytes=16 * 1024 * 1024),
        cost_estimate=pl.CostEstimate(flops=0, bytes_accessed=4 << 20, transcendentals=0),
    )(pos, *received)


def on_device(
    features, block_row, block_col, block_count, block_values, w_self, w_neigh, cotangent
):
    rows_part = features.shape[1]
    depth, width = cotangent.shape
    rim = REACH * BLK
    chunk = width // BLK
    pos = lax.axis_index("feat").astype(jnp.int32)[None]
    lists = list_step(block_row[0], block_col[0], block_count, pos, chunk)
    w_in = jnp.concatenate([w_self.T, w_neigh.T], axis=1)
    w_out = jnp.concatenate([w_self, w_neigh], axis=0)
    pieces = lax.axis_size("feat")
    received = list(cut_step(pos, features, pieces))
    for step in sorted(range(1, pieces), key=lambda step: (abs(2 * step - pieces), step)):
        received[step] = shifted(received[step], "feat", step)
    own, head, tail = join_step(pos, received, rim)
    before = shifted(tail, RING, 1)
    after = shifted(head, RING, -1)
    agg = before_step(lists, own, block_values)
    left, right, terms, both = local_step(
        lists, agg, own, before, after, block_values, w_in, w_out, cotangent
    )
    plane, line = lax.axis_size(PLANE), lax.axis_size(LINE)
    share = 2 * depth // plane
    from_next = shifted(left, RING, -1)
    from_prev = shifted(right, RING, 1)
    parts = lax.all_to_all(terms, PLANE, split_axis=0, concat_axis=0, tiled=True)
    partial = parts.reshape(plane, share, depth).sum(0).astype(jnp.bfloat16)
    middle = after_step(lists, both, block_values)
    partial, middle = lax.optimization_barrier((partial, middle))
    copies = jnp.broadcast_to(partial[None], (line, share, depth))
    copies = lax.all_to_all(copies, LINE, split_axis=0, concat_axis=0, tiled=True)
    factor = 1.0 / math.sqrt(rows_part * lax.axis_size(DOM))
    grads = copies.reshape(line, share, depth).astype(jnp.float32).sum(0) * factor
    total = total_step(middle, from_prev, from_next)
    total, grads = lax.optimization_barrier((total, grads.astype(jnp.bfloat16)))
    feature_grad = lax.all_to_all(total, "feat", split_axis=0, concat_axis=1, tiled=True)
    grads = collected(grads)
    return (feature_grad, grads[:depth], grads[depth:])


def solution(mesh):
    fine = Mesh(mesh.devices.reshape(2, 4, 4, 2, 8), RING)
    return jax.shard_map(
        on_device,
        mesh=fine,
        in_specs=(
            P("feat", DOM),
            P(DOM, None),
            P(DOM, None),
            P(DOM),
            P(DOM, None, None),
            P(),
            P(),
            P(None, RING),
        ),
        out_specs=(P("feat", DOM), P(), P()),
        check_vma=False,
    )
```

```python
import functools
import math

import jax
import jax.numpy as jnp
from jax import lax
from jax.experimental import pallas as pl
from jax.experimental.pallas import tpu as pltpu
from jax.sharding import Mesh, PartitionSpec as P

BLK = 128
REACH = 8
DOM = ("zh", "y", "x", "core")
PLANE = ("y", "x", "core")
LINE = ("zh", "feat")
RING = DOM + ("feat",)


def shifted(shard, axis, by):
    count = lax.axis_size(axis)
    return lax.ppermute(shard, axis, [(i, (i + by) % count) for i in range(count)])


def collected(rows):
    for axis in reversed(PLANE):
        count = lax.axis_size(axis)
        apart = 1
        while apart < count:
            other = lax.ppermute(rows, axis, [(i, i ^ apart) for i in range(count)])
            second = (lax.axis_index(axis) & apart) != 0
            rows = jnp.concatenate(
                [jnp.where(second, other, rows), jnp.where(second, rows, other)], axis=0
            )
            apart *= 2
    return rows


def tiles_of(width, tile):
    return [(at, min(tile, width - at)) for at in range(0, width, tile)]


SMEM = pl.BlockSpec(memory_space=pltpu.SMEM)
VMEM = pl.BlockSpec(memory_space=pltpu.VMEM)
LEFT, OWN, RIGHT = range(3)


def list_kernel(chunk, rows_ref, cols_ref, count_ref, pos_ref, used_ref, slot_ref, row_ref, col_ref):
    slots = rows_ref.shape[0]
    first = pos_ref[0] * chunk
    for kind in range(3):
        used_ref[kind] = 0

    def step(slot, carry):
        row = rows_ref[slot] - first

        @pl.when((row >= 0) & (row < chunk))
        def _():
            col = cols_ref[slot] - first - REACH
            kind = jnp.where(col < 0, LEFT, jnp.where(col < chunk, OWN, RIGHT))
            base = jnp.where(col < 0, REACH, jnp.where(col < chunk, 0, -chunk))
            at = kind * slots + used_ref[kind]
            slot_ref[at] = slot
            row_ref[at] = row
            col_ref[at] = col + base
            used_ref[kind] = used_ref[kind] + 1

        return carry

    lax.fori_loop(0, jnp.minimum(count_ref[0], slots), step, 0)


def list_step(rows, cols, count, pos, chunk):
    table = jax.ShapeDtypeStruct((3 * rows.shape[0],), jnp.int32)
    return pl.pallas_call(
        functools.partial(list_kernel, chunk),
        out_shape=(jax.ShapeDtypeStruct((3,), jnp.int32), table, table, table),
        in_specs=[SMEM] * 4,
        out_specs=(SMEM,) * 4,
        cost_estimate=pl.CostEstimate(flops=0, bytes_accessed=4096, transcendentals=0),
    )(rows, cols, count, pos)


def block(index):
    return pl.ds(pl.multiple_of(index * BLK, BLK), BLK)


def add_slots(lists, kind, source, into, values, forward):
    used_ref, slot_ref, row_ref, col_ref = lists
    base = kind * (slot_ref.shape[0] // 3)
    count = used_ref[kind]

    def some(indices):
        products = []
        for at in indices:
            read = col_ref[at] if forward else row_ref[at]
            products.append(
                lax.dot_general(
                    source[:, block(read)],
                    values[slot_ref[at]],
                    (((1,), (1 if forward else 0,)), ((), ())),
                    preferred_element_type=jnp.float32,
                )
            )
        for at, product in zip(indices, products):
            write = row_ref[at] if forward else col_ref[at]
            into[:, block(write)] += product

    def pair(step, carry):
        some([base + 2 * step, base + 2 * step + 1])
        return carry

    lax.fori_loop(0, lax.div(count, 2), pair, 0)

    @pl.when(lax.rem(count, 2) == 1)
    def _():
        some([base + count - 1])


def before_kernel(*refs):
    lists, (own_ref, values_ref, agg_ref) = refs[:4], refs[4:]
    agg_ref[...] = jnp.zeros_like(agg_ref)
    add_slots(lists, OWN, own_ref, agg_ref, values_ref, True)


def before_step(lists, own, values):
    return pl.pallas_call(
        before_kernel,
        out_shape=jax.ShapeDtypeStruct(own.shape, jnp.float32),
        in_specs=[SMEM] * 4 + [VMEM] * 2,
        out_specs=VMEM,
        compiler_params=pltpu.CompilerParams(vmem_limit_bytes=24 * 1024 * 1024),
        cost_estimate=pl.CostEstimate(flops=1 << 28, bytes_accessed=4 << 20, transcendentals=0),
    )(*lists, own, values)


def local_kernel(*refs):
    lists = refs[:4]
    (agg_ref, own_ref, before_ref, after_ref, values_ref, w_in_ref, w_out_ref, cot_ref) = refs[4:12]
    left_ref, right_ref, terms_ref, both_ref, stacked, delta, agg, scat = refs[12:]
    depth, width = own_ref.shape
    agg[...] = agg_ref[...]
    add_slots(lists, LEFT, before_ref, agg, values_ref, True)
    add_slots(lists, RIGHT, after_ref, agg, values_ref, True)
    for at, size in tiles_of(width, 256):
        part = slice(at, at + size)
        stacked[:depth, part] = own_ref[:, part]
        stacked[depth:, part] = agg[:, part].astype(jnp.bfloat16)
        preact = jnp.dot(w_in_ref[...], stacked[:, part], preferred_element_type=jnp.float32)
        sigma = 1.0 / (1.0 + jnp.exp(-preact))
        slope = sigma * (1.0 + preact * (1.0 - sigma))
        delta[:, part] = (cot_ref[:, part].astype(jnp.float32) * slope).astype(jnp.bfloat16)
        both = jnp.dot(w_out_ref[...], delta[:, part], preferred_element_type=jnp.float32)
        both_ref[:, part] = both.astype(jnp.bfloat16)
    agg_grad = both_ref.at[pl.ds(depth, depth)]
    for kind, out_ref in ((LEFT, left_ref), (RIGHT, right_ref)):
        scat[...] = jnp.zeros_like(scat)
        add_slots(lists, kind, agg_grad, scat, values_ref, False)
        out_ref[...] = scat[...].astype(jnp.bfloat16)
    terms_ref[...] = lax.dot_general(
        stacked[...], delta[...], (((1,), (1,)), ((), ())), preferred_element_type=jnp.float32
    )


def local_step(lists, agg, own, before, after, values, w_in, w_out, cot):
    depth, width = own.shape
    rim = before.shape[1]
    return pl.pallas_call(
        local_kernel,
        out_shape=(
            jax.ShapeDtypeStruct((depth, rim), jnp.bfloat16),
            jax.ShapeDtypeStruct((depth, rim), jnp.bfloat16),
            jax.ShapeDtypeStruct((2 * depth, depth), jnp.float32),
            jax.ShapeDtypeStruct((2 * depth, width), jnp.bfloat16),
        ),
        in_specs=[SMEM] * 4 + [VMEM] * 8,
        out_specs=(VMEM,) * 4,
        scratch_shapes=[
            pltpu.VMEM((2 * depth, width), jnp.bfloat16),
            pltpu.VMEM((depth, width), jnp.bfloat16),
            pltpu.VMEM((depth, width), jnp.float32),
            pltpu.VMEM((depth, rim), jnp.float32),
        ],
        compiler_params=pltpu.CompilerParams(vmem_limit_bytes=40 * 1024 * 1024),
        cost_estimate=pl.CostEstimate(
            flops=12 * depth * depth * width, bytes_accessed=8 << 20, transcendentals=depth * width
        ),
    )(*lists, agg, own, before, after, values, w_in, w_out, cot)


def after_kernel(*refs):
    lists, (both_ref, values_ref, middle_ref) = refs[:4], refs[4:]
    depth = middle_ref.shape[0]
    middle_ref[...] = both_ref[:depth].astype(jnp.float32)
    add_slots(lists, OWN, both_ref.at[pl.ds(depth, depth)], middle_ref, values_ref, False)


def after_step(lists, both, values):
    return pl.pallas_call(
        after_kernel,
        out_shape=jax.ShapeDtypeStruct((both.shape[0] // 2, both.shape[1]), jnp.float32),
        in_specs=[SMEM] * 4 + [VMEM] * 2,
        out_specs=VMEM,
        compiler_params=pltpu.CompilerParams(vmem_limit_bytes=24 * 1024 * 1024),
        cost_estimate=pl.CostEstimate(flops=1 << 28, bytes_accessed=6 << 20, transcendentals=0),
    )(*lists, both, values)


def total_kernel(middle_ref, prev_ref, next_ref, out_ref):
    width, rim = middle_ref.shape[1], prev_ref.shape[1]
    edges = sorted({0, min(rim, width - rim), max(rim, width - rim), width})
    for at, end in zip(edges, edges[1:]):
        part = middle_ref[:, at:end]
        if at < rim:
            part = part + prev_ref[:, at:end].astype(jnp.float32)
        if at >= width - rim:
            here = at - (width - rim)
            part = part + next_ref[:, here : here + end - at].astype(jnp.float32)
        out_ref[:, at:end] = part.astype(jnp.bfloat16)


def total_step(middle, from_prev, from_next):
    return pl.pallas_call(
        total_kernel,
        out_shape=jax.ShapeDtypeStruct(middle.shape, jnp.bfloat16),
        in_specs=[VMEM] * 3,
        out_specs=VMEM,
        compiler_params=pltpu.CompilerParams(vmem_limit_bytes=24 * 1024 * 1024),
        cost_estimate=pl.CostEstimate(flops=0, bytes_accessed=4 << 20, transcendentals=0),
    )(middle, from_prev, from_next)


def cut_kernel(pos_ref, features_ref, *refs):
    piece_refs, sems = refs[:-1], refs[-1]
    pieces, width = len(piece_refs), piece_refs[0].shape[1]
    copies = []
    for step, piece_ref in enumerate(piece_refs):
        dest = lax.rem(pos_ref[0] + step, pieces)
        part = pl.ds(pl.multiple_of(dest * width, BLK), width)
        copies.append(pltpu.make_async_copy(features_ref.at[:, part], piece_ref, sems.at[step]))
    for copy in copies:
        copy.start()
    for copy in copies:
        copy.wait()


def cut_step(pos, features, pieces):
    height, width = features.shape[0], features.shape[1] // pieces
    return pl.pallas_call(
        cut_kernel,
        out_shape=(jax.ShapeDtypeStruct((height, width), features.dtype),) * pieces,
        in_specs=[SMEM, pl.BlockSpec(memory_space=pl.ANY)],
        out_specs=(VMEM,) * pieces,
        scratch_shapes=[pltpu.SemaphoreType.DMA((pieces,))],
        compiler_params=pltpu.CompilerParams(vmem_limit_bytes=16 * 1024 * 1024),
        cost_estimate=pl.CostEstimate(flops=0, bytes_accessed=2 << 20, transcendentals=0),
    )(pos, features)


def join_kernel(pos_ref, *refs):
    piece_refs, (own_ref, head_ref, tail_ref) = refs[:-3], refs[-3:]
    pieces = len(piece_refs)
    height, width = piece_refs[0].shape
    rim = head_ref.shape[1]
    for step, piece_ref in enumerate(piece_refs):
        source = lax.rem(pos_ref[0] + pieces - step, pieces)
        rows = pl.ds(pl.multiple_of(source * height, height), height)
        own_ref[rows, :] = piece_ref[...]
        head_ref[rows, :] = piece_ref[:, :rim]
        tail_ref[rows, :] = piece_ref[:, width - rim :]


def join_step(pos, received, rim):
    pieces = len(received)
    height, width = received[0].shape
    depth, kind = pieces * height, received[0].dtype
    edge = jax.ShapeDtypeStruct((depth, rim), kind)
    return pl.pallas_call(
        join_kernel,
        out_shape=(jax.ShapeDtypeStruct((depth, width), kind), edge, edge),
        in_specs=[SMEM] + [VMEM] * pieces,
        out_specs=(VMEM,) * 3,
        compiler_params=pltpu.CompilerParams(vmem_limit_bytes=16 * 1024 * 1024),
        cost_estimate=pl.CostEstimate(flops=0, bytes_accessed=4 << 20, transcendentals=0),
    )(pos, *received)


def on_device(
    features, block_row, block_col, block_count, block_values, w_self, w_neigh, cotangent
):
    rows_part = features.shape[1]
    depth, width = cotangent.shape
    rim = REACH * BLK
    chunk = width // BLK
    pos = lax.axis_index("feat").astype(jnp.int32)[None]
    lists = list_step(block_row[0], block_col[0], block_count, pos, chunk)
    w_in = jnp.concatenate([w_self.T, w_neigh.T], axis=1)
    w_out = jnp.concatenate([w_self, w_neigh], axis=0)
    pieces = lax.axis_size("feat")
    received = list(cut_step(pos, features, pieces))
    for step in sorted(range(1, pieces), key=lambda step: (abs(2 * step - pieces), step)):
        received[step] = shifted(received[step], "feat", step)
    own, head, tail = join_step(pos, received, rim)
    before = shifted(tail, RING, 1)
    after = shifted(head, RING, -1)
    agg = before_step(lists, own, block_values)
    left, right, terms, both = local_step(
        lists, agg, own, before, after, block_values, w_in, w_out, cotangent
    )
    plane, line = lax.axis_size(PLANE), lax.axis_size(LINE)
    share = 2 * depth // plane
    from_next = shifted(left, RING, -1)
    from_prev = shifted(right, RING, 1)
    parts = lax.all_to_all(terms, PLANE, split_axis=0, concat_axis=0, tiled=True)
    partial = parts.reshape(plane, share, depth).sum(0).astype(jnp.bfloat16)
    partial, used = lax.optimization_barrier((partial, lists[0]))
    middle = after_step([used, *lists[1:]], both, block_values)
    copies = jnp.broadcast_to(partial[None], (line, share, depth))
    copies = lax.all_to_all(copies, LINE, split_axis=0, concat_axis=0, tiled=True)
    factor = 1.0 / math.sqrt(rows_part * lax.axis_size(DOM))
    grads = copies.reshape(line, share, depth).astype(jnp.float32).sum(0) * factor
    total = total_step(middle, from_prev, from_next)
    total, grads = lax.optimization_barrier((total, grads.astype(jnp.bfloat16)))
    feature_grad = lax.all_to_all(total, "feat", split_axis=0, concat_axis=1, tiled=True)
    grads = collected(grads)
    return (feature_grad, grads[:depth], grads[depth:])


def solution(mesh):
    fine = Mesh(mesh.devices.reshape(2, 4, 4, 2, 8), RING)
    return jax.shard_map(
        on_device,
        mesh=fine,
        in_specs=(
            P("feat", DOM),
            P(DOM, None),
            P(DOM, None),
            P(DOM),
            P(DOM, None, None),
            P(),
            P(),
            P(None, RING),
        ),
        out_specs=(P("feat", DOM), P(), P()),
        check_vma=False,
    )
```

```python
import functools
import math

import jax
import jax.numpy as jnp
from jax import lax
from jax.experimental import pallas as pl
from jax.experimental.pallas import tpu as pltpu
from jax.sharding import Mesh, PartitionSpec as P

BLK = 128
REACH = 8
DOM = ("zh", "y", "x", "core")
PLANE = ("y", "x", "core")
LINE = ("zh", "feat")
RING = DOM + ("feat",)


def shifted(shard, axis, by):
    count = lax.axis_size(axis)
    return lax.ppermute(shard, axis, [(i, (i + by) % count) for i in range(count)])


def collected(rows):
    for axis in reversed(PLANE):
        count = lax.axis_size(axis)
        apart = 1
        while apart < count:
            other = lax.ppermute(rows, axis, [(i, i ^ apart) for i in range(count)])
            second = (lax.axis_index(axis) & apart) != 0
            rows = jnp.concatenate(
                [jnp.where(second, other, rows), jnp.where(second, rows, other)], axis=0
            )
            apart *= 2
    return rows


def tiles_of(width, tile):
    return [(at, min(tile, width - at)) for at in range(0, width, tile)]


SMEM = pl.BlockSpec(memory_space=pltpu.SMEM)
VMEM = pl.BlockSpec(memory_space=pltpu.VMEM)
LEFT, OWN, RIGHT = range(3)


def list_kernel(chunk, rows_ref, cols_ref, count_ref, pos_ref, used_ref, slot_ref, row_ref, col_ref):
    slots = rows_ref.shape[0]
    first = pos_ref[0] * chunk
    for kind in range(3):
        used_ref[kind] = 0

    def step(slot, carry):
        row = rows_ref[slot] - first

        @pl.when((row >= 0) & (row < chunk))
        def _():
            col = cols_ref[slot] - first - REACH
            kind = jnp.where(col < 0, LEFT, jnp.where(col < chunk, OWN, RIGHT))
            base = jnp.where(col < 0, REACH, jnp.where(col < chunk, 0, -chunk))
            at = kind * slots + used_ref[kind]
            slot_ref[at] = slot
            row_ref[at] = row
            col_ref[at] = col + base
            used_ref[kind] = used_ref[kind] + 1

        return carry

    lax.fori_loop(0, jnp.minimum(count_ref[0], slots), step, 0)


def list_step(rows, cols, count, pos, chunk):
    table = jax.ShapeDtypeStruct((3 * rows.shape[0],), jnp.int32)
    return pl.pallas_call(
        functools.partial(list_kernel, chunk),
        out_shape=(jax.ShapeDtypeStruct((3,), jnp.int32), table, table, table),
        in_specs=[SMEM] * 4,
        out_specs=(SMEM,) * 4,
        cost_estimate=pl.CostEstimate(flops=0, bytes_accessed=4096, transcendentals=0),
    )(rows, cols, count, pos)


def block(index):
    return pl.ds(pl.multiple_of(index * BLK, BLK), BLK)


def add_slots(lists, kind, source, into, values, forward):
    used_ref, slot_ref, row_ref, col_ref = lists
    base = kind * (slot_ref.shape[0] // 3)
    count = used_ref[kind]

    def some(indices):
        products = []
        for at in indices:
            read = col_ref[at] if forward else row_ref[at]
            products.append(
                lax.dot_general(
                    source[:, block(read)],
                    values[slot_ref[at]],
                    (((1,), (1 if forward else 0,)), ((), ())),
                    preferred_element_type=jnp.float32,
                )
            )
        for at, product in zip(indices, products):
            write = row_ref[at] if forward else col_ref[at]
            into[:, block(write)] += product

    def pair(step, carry):
        some([base + 2 * step, base + 2 * step + 1])
        return carry

    lax.fori_loop(0, lax.div(count, 2), pair, 0)

    @pl.when(lax.rem(count, 2) == 1)
    def _():
        some([base + count - 1])


def before_kernel(*refs):
    lists, (own_ref, values_ref, agg_ref) = refs[:4], refs[4:]
    agg_ref[...] = jnp.zeros_like(agg_ref)
    add_slots(lists, OWN, own_ref, agg_ref, values_ref, True)


def before_step(lists, own, values):
    return pl.pallas_call(
        before_kernel,
        out_shape=jax.ShapeDtypeStruct(own.shape, jnp.float32),
        in_specs=[SMEM] * 4 + [VMEM] * 2,
        out_specs=VMEM,
        compiler_params=pltpu.CompilerParams(vmem_limit_bytes=24 * 1024 * 1024),
        cost_estimate=pl.CostEstimate(flops=1 << 28, bytes_accessed=4 << 20, transcendentals=0),
    )(*lists, own, values)


def local_kernel(*refs):
    lists = refs[:4]
    (agg_ref, own_ref, before_ref, after_ref, values_ref, w_in_ref, w_out_ref, cot_ref) = refs[4:12]
    left_ref, right_ref, terms_ref, both_ref, stacked, delta, agg, scat = refs[12:]
    depth, width = own_ref.shape
    agg[...] = agg_ref[...]
    add_slots(lists, LEFT, before_ref, agg, values_ref, True)
    add_slots(lists, RIGHT, after_ref, agg, values_ref, True)
    for at, size in tiles_of(width, 256):
        part = slice(at, at + size)
        stacked[:depth, part] = own_ref[:, part]
        stacked[depth:, part] = agg[:, part].astype(jnp.bfloat16)
        preact = jnp.dot(w_in_ref[...], stacked[:, part], preferred_element_type=jnp.float32)
        sigma = 1.0 / (1.0 + jnp.exp(-preact))
        slope = sigma * (1.0 + preact * (1.0 - sigma))
        delta[:, part] = (cot_ref[:, part].astype(jnp.float32) * slope).astype(jnp.bfloat16)
        both = jnp.dot(w_out_ref[...], delta[:, part], preferred_element_type=jnp.float32)
        both_ref[:, part] = both.astype(jnp.bfloat16)
    agg_grad = both_ref.at[pl.ds(depth, depth)]
    for kind, out_ref in ((LEFT, left_ref), (RIGHT, right_ref)):
        scat[...] = jnp.zeros_like(scat)
        add_slots(lists, kind, agg_grad, scat, values_ref, False)
        out_ref[...] = scat[...].astype(jnp.bfloat16)
    terms_ref[...] = lax.dot_general(
        stacked[...], delta[...], (((1,), (1,)), ((), ())), preferred_element_type=jnp.float32
    )


def local_step(lists, agg, own, before, after, values, w_in, w_out, cot):
    depth, width = own.shape
    rim = before.shape[1]
    return pl.pallas_call(
        local_kernel,
        out_shape=(
            jax.ShapeDtypeStruct((depth, rim), jnp.bfloat16),
            jax.ShapeDtypeStruct((depth, rim), jnp.bfloat16),
            jax.ShapeDtypeStruct((2 * depth, depth), jnp.float32),
            jax.ShapeDtypeStruct((2 * depth, width), jnp.bfloat16),
        ),
        in_specs=[SMEM] * 4 + [VMEM] * 8,
        out_specs=(VMEM,) * 4,
        scratch_shapes=[
            pltpu.VMEM((2 * depth, width), jnp.bfloat16),
            pltpu.VMEM((depth, width), jnp.bfloat16),
            pltpu.VMEM((depth, width), jnp.float32),
            pltpu.VMEM((depth, rim), jnp.float32),
        ],
        compiler_params=pltpu.CompilerParams(vmem_limit_bytes=40 * 1024 * 1024),
        cost_estimate=pl.CostEstimate(
            flops=12 * depth * depth * width, bytes_accessed=8 << 20, transcendentals=depth * width
        ),
    )(*lists, agg, own, before, after, values, w_in, w_out, cot)


def after_kernel(*refs):
    lists, (both_ref, values_ref, middle_ref) = refs[:4], refs[4:]
    depth = middle_ref.shape[0]
    middle_ref[...] = both_ref[:depth].astype(jnp.float32)
    add_slots(lists, OWN, both_ref.at[pl.ds(depth, depth)], middle_ref, values_ref, False)


def after_step(lists, both, values):
    return pl.pallas_call(
        after_kernel,
        out_shape=jax.ShapeDtypeStruct((both.shape[0] // 2, both.shape[1]), jnp.float32),
        in_specs=[SMEM] * 4 + [VMEM] * 2,
        out_specs=VMEM,
        compiler_params=pltpu.CompilerParams(vmem_limit_bytes=24 * 1024 * 1024),
        cost_estimate=pl.CostEstimate(flops=1 << 28, bytes_accessed=6 << 20, transcendentals=0),
    )(*lists, both, values)


def total_kernel(middle_ref, prev_ref, next_ref, out_ref):
    width, rim = middle_ref.shape[1], prev_ref.shape[1]
    edges = sorted({0, min(rim, width - rim), max(rim, width - rim), width})
    for at, end in zip(edges, edges[1:]):
        part = middle_ref[:, at:end]
        if at < rim:
            part = part + prev_ref[:, at:end].astype(jnp.float32)
        if at >= width - rim:
            here = at - (width - rim)
            part = part + next_ref[:, here : here + end - at].astype(jnp.float32)
        out_ref[:, at:end] = part.astype(jnp.bfloat16)


def total_step(middle, from_prev, from_next):
    return pl.pallas_call(
        total_kernel,
        out_shape=jax.ShapeDtypeStruct(middle.shape, jnp.bfloat16),
        in_specs=[VMEM] * 3,
        out_specs=VMEM,
        compiler_params=pltpu.CompilerParams(vmem_limit_bytes=24 * 1024 * 1024),
        cost_estimate=pl.CostEstimate(flops=0, bytes_accessed=4 << 20, transcendentals=0),
    )(middle, from_prev, from_next)


def cut_kernel(pos_ref, features_ref, *refs):
    piece_refs, sems = refs[:-1], refs[-1]
    pieces, width = len(piece_refs), piece_refs[0].shape[1]
    copies = []
    for step, piece_ref in enumerate(piece_refs):
        dest = lax.rem(pos_ref[0] + step, pieces)
        part = pl.ds(pl.multiple_of(dest * width, BLK), width)
        copies.append(pltpu.make_async_copy(features_ref.at[:, part], piece_ref, sems.at[step]))
    for copy in copies:
        copy.start()
    for copy in copies:
        copy.wait()


def cut_step(pos, features, pieces):
    height, width = features.shape[0], features.shape[1] // pieces
    return pl.pallas_call(
        cut_kernel,
        out_shape=(jax.ShapeDtypeStruct((height, width), features.dtype),) * pieces,
        in_specs=[SMEM, pl.BlockSpec(memory_space=pl.ANY)],
        out_specs=(VMEM,) * pieces,
        scratch_shapes=[pltpu.SemaphoreType.DMA((pieces,))],
        compiler_params=pltpu.CompilerParams(vmem_limit_bytes=16 * 1024 * 1024),
        cost_estimate=pl.CostEstimate(flops=0, bytes_accessed=2 << 20, transcendentals=0),
    )(pos, features)


def join_kernel(pos_ref, *refs):
    piece_refs, (own_ref, head_ref, tail_ref) = refs[:-3], refs[-3:]
    pieces = len(piece_refs)
    height, width = piece_refs[0].shape
    rim = head_ref.shape[1]
    for step, piece_ref in enumerate(piece_refs):
        source = lax.rem(pos_ref[0] + pieces - step, pieces)
        rows = pl.ds(pl.multiple_of(source * height, height), height)
        own_ref[rows, :] = piece_ref[...]
        head_ref[rows, :] = piece_ref[:, :rim]
        tail_ref[rows, :] = piece_ref[:, width - rim :]


def join_step(pos, received, rim):
    pieces = len(received)
    height, width = received[0].shape
    depth, kind = pieces * height, received[0].dtype
    edge = jax.ShapeDtypeStruct((depth, rim), kind)
    return pl.pallas_call(
        join_kernel,
        out_shape=(jax.ShapeDtypeStruct((depth, width), kind), edge, edge),
        in_specs=[SMEM] + [VMEM] * pieces,
        out_specs=(VMEM,) * 3,
        compiler_params=pltpu.CompilerParams(vmem_limit_bytes=16 * 1024 * 1024),
        cost_estimate=pl.CostEstimate(flops=0, bytes_accessed=4 << 20, transcendentals=0),
    )(pos, *received)


def on_device(
    features, block_row, block_col, block_count, block_values, w_self, w_neigh, cotangent
):
    rows_part = features.shape[1]
    depth, width = cotangent.shape
    rim = REACH * BLK
    chunk = width // BLK
    pos = lax.axis_index("feat").astype(jnp.int32)[None]
    lists = list_step(block_row[0], block_col[0], block_count, pos, chunk)
    w_in = jnp.concatenate([w_self.T, w_neigh.T], axis=1)
    w_out = jnp.concatenate([w_self, w_neigh], axis=0)
    pieces = lax.axis_size("feat")
    received = list(cut_step(pos, features, pieces))
    far = sorted(range(1, pieces), key=lambda step: (abs(2 * step - pieces), step))
    half = (pieces - 1) // 2 + 1
    mixed = [step for pair in zip(far[:half], far[half:] + [0]) for step in pair if step]
    for step in mixed:
        received[step] = shifted(received[step], "feat", step)
    own, head, tail = join_step(pos, received, rim)
    before = shifted(tail, RING, 1)
    after = shifted(head, RING, -1)
    agg = before_step(lists, own, block_values)
    left, right, terms, both = local_step(
        lists, agg, own, before, after, block_values, w_in, w_out, cotangent
    )
    plane, line = lax.axis_size(PLANE), lax.axis_size(LINE)
    share = 2 * depth // plane
    from_next = shifted(left, RING, -1)
    from_prev = shifted(right, RING, 1)
    parts = lax.all_to_all(terms, PLANE, split_axis=0, concat_axis=0, tiled=True)
    partial = parts.reshape(plane, share, depth).sum(0).astype(jnp.bfloat16)
    partial, used = lax.optimization_barrier((partial, lists[0]))
    middle = after_step([used, *lists[1:]], both, block_values)
    copies = jnp.broadcast_to(partial[None], (line, share, depth))
    copies = lax.all_to_all(copies, LINE, split_axis=0, concat_axis=0, tiled=True)
    factor = 1.0 / math.sqrt(rows_part * lax.axis_size(DOM))
    grads = copies.reshape(line, share, depth).astype(jnp.float32).sum(0) * factor
    total = total_step(middle, from_prev, from_next)
    total, grads = lax.optimization_barrier((total, grads.astype(jnp.bfloat16)))
    feature_grad = lax.all_to_all(total, "feat", split_axis=0, concat_axis=1, tiled=True)
    grads = collected(grads)
    return (feature_grad, grads[:depth], grads[depth:])


def solution(mesh):
    fine = Mesh(mesh.devices.reshape(2, 4, 4, 2, 8), RING)
    return jax.shard_map(
        on_device,
        mesh=fine,
        in_specs=(
            P("feat", DOM),
            P(DOM, None),
            P(DOM, None),
            P(DOM),
            P(DOM, None, None),
            P(),
            P(),
            P(None, RING),
        ),
        out_specs=(P("feat", DOM), P(), P()),
        check_vma=False,
    )
```

```python
import functools
import math

import jax
import jax.numpy as jnp
from jax import lax
from jax.experimental import pallas as pl
from jax.experimental.pallas import tpu as pltpu
from jax.sharding import Mesh, PartitionSpec as P

BLK = 128
REACH = 8
DOM = ("zh", "y", "x", "core")
PLANE = ("y", "x", "core")
LINE = ("zh", "feat")
RING = DOM + ("feat",)


def shifted(shard, axis, by):
    count = lax.axis_size(axis)
    return lax.ppermute(shard, axis, [(i, (i + by) % count) for i in range(count)])


def collected(rows):
    for axis in reversed(PLANE):
        count = lax.axis_size(axis)
        apart = 1
        while apart < count:
            other = lax.ppermute(rows, axis, [(i, i ^ apart) for i in range(count)])
            second = (lax.axis_index(axis) & apart) != 0
            rows = jnp.concatenate(
                [jnp.where(second, other, rows), jnp.where(second, rows, other)], axis=0
            )
            apart *= 2
    return rows


def tiles_of(width, tile):
    return [(at, min(tile, width - at)) for at in range(0, width, tile)]


SMEM = pl.BlockSpec(memory_space=pltpu.SMEM)
VMEM = pl.BlockSpec(memory_space=pltpu.VMEM)
LEFT, OWN, RIGHT = range(3)


def list_kernel(chunk, rows_ref, cols_ref, count_ref, pos_ref, used_ref, slot_ref, row_ref, col_ref):
    slots = rows_ref.shape[0]
    first = pos_ref[0] * chunk
    for kind in range(3):
        used_ref[kind] = 0

    def step(slot, carry):
        row = rows_ref[slot] - first

        @pl.when((row >= 0) & (row < chunk))
        def _():
            col = cols_ref[slot] - first - REACH
            kind = jnp.where(col < 0, LEFT, jnp.where(col < chunk, OWN, RIGHT))
            base = jnp.where(col < 0, REACH, jnp.where(col < chunk, 0, -chunk))
            at = kind * slots + used_ref[kind]
            slot_ref[at] = slot
            row_ref[at] = row
            col_ref[at] = col + base
            used_ref[kind] = used_ref[kind] + 1

        return carry

    lax.fori_loop(0, jnp.minimum(count_ref[0], slots), step, 0)


def list_step(rows, cols, count, pos, chunk):
    table = jax.ShapeDtypeStruct((3 * rows.shape[0],), jnp.int32)
    return pl.pallas_call(
        functools.partial(list_kernel, chunk),
        out_shape=(jax.ShapeDtypeStruct((3,), jnp.int32), table, table, table),
        in_specs=[SMEM] * 4,
        out_specs=(SMEM,) * 4,
        cost_estimate=pl.CostEstimate(flops=0, bytes_accessed=4096, transcendentals=0),
    )(rows, cols, count, pos)


def block(index):
    return pl.ds(pl.multiple_of(index * BLK, BLK), BLK)


def add_slots(lists, kind, source, into, values, forward):
    used_ref, slot_ref, row_ref, col_ref = lists
    base = kind * (slot_ref.shape[0] // 3)
    count = used_ref[kind]

    def some(indices):
        products = []
        for at in indices:
            read = col_ref[at] if forward else row_ref[at]
            products.append(
                lax.dot_general(
                    source[:, block(read)],
                    values[slot_ref[at]],
                    (((1,), (1 if forward else 0,)), ((), ())),
                    preferred_element_type=jnp.float32,
                )
            )
        for at, product in zip(indices, products):
            write = row_ref[at] if forward else col_ref[at]
            into[:, block(write)] += product

    def pair(step, carry):
        some([base + 2 * step, base + 2 * step + 1])
        return carry

    lax.fori_loop(0, lax.div(count, 2), pair, 0)

    @pl.when(lax.rem(count, 2) == 1)
    def _():
        some([base + count - 1])


def before_kernel(*refs):
    lists, (own_ref, values_ref, agg_ref) = refs[:4], refs[4:]
    agg_ref[...] = jnp.zeros_like(agg_ref)
    add_slots(lists, OWN, own_ref, agg_ref, values_ref, True)


def before_step(lists, own, values):
    return pl.pallas_call(
        before_kernel,
        out_shape=jax.ShapeDtypeStruct(own.shape, jnp.float32),
        in_specs=[SMEM] * 4 + [VMEM] * 2,
        out_specs=VMEM,
        compiler_params=pltpu.CompilerParams(vmem_limit_bytes=24 * 1024 * 1024),
        cost_estimate=pl.CostEstimate(flops=1 << 28, bytes_accessed=4 << 20, transcendentals=0),
    )(*lists, own, values)


def local_kernel(*refs):
    lists = refs[:4]
    (agg_ref, own_ref, before_ref, after_ref, values_ref, w_in_ref, w_out_ref, cot_ref) = refs[4:12]
    left_ref, right_ref, terms_ref, both_ref, stacked, delta, agg, scat = refs[12:]
    depth, width = own_ref.shape
    agg[...] = agg_ref[...]
    add_slots(lists, LEFT, before_ref, agg, values_ref, True)
    add_slots(lists, RIGHT, after_ref, agg, values_ref, True)
    for at, size in tiles_of(width, 256):
        part = slice(at, at + size)
        stacked[:depth, part] = own_ref[:, part]
        stacked[depth:, part] = agg[:, part].astype(jnp.bfloat16)
        preact = jnp.dot(w_in_ref[...], stacked[:, part], preferred_element_type=jnp.float32)
        sigma = 1.0 / (1.0 + jnp.exp(-preact))
        slope = sigma * (1.0 + preact * (1.0 - sigma))
        delta[:, part] = (cot_ref[:, part].astype(jnp.float32) * slope).astype(jnp.bfloat16)
        both = jnp.dot(w_out_ref[...], delta[:, part], preferred_element_type=jnp.float32)
        both_ref[:, part] = both.astype(jnp.bfloat16)
    agg_grad = both_ref.at[pl.ds(depth, depth)]
    for kind, out_ref in ((LEFT, left_ref), (RIGHT, right_ref)):
        scat[...] = jnp.zeros_like(scat)
        add_slots(lists, kind, agg_grad, scat, values_ref, False)
        out_ref[...] = scat[...].astype(jnp.bfloat16)
    terms_ref[...] = lax.dot_general(
        stacked[...], delta[...], (((1,), (1,)), ((), ())), preferred_element_type=jnp.float32
    )


def local_step(lists, agg, own, before, after, values, w_in, w_out, cot):
    depth, width = own.shape
    rim = before.shape[1]
    return pl.pallas_call(
        local_kernel,
        out_shape=(
            jax.ShapeDtypeStruct((depth, rim), jnp.bfloat16),
            jax.ShapeDtypeStruct((depth, rim), jnp.bfloat16),
            jax.ShapeDtypeStruct((2 * depth, depth), jnp.float32),
            jax.ShapeDtypeStruct((2 * depth, width), jnp.bfloat16),
        ),
        in_specs=[SMEM] * 4 + [VMEM] * 8,
        out_specs=(VMEM,) * 4,
        scratch_shapes=[
            pltpu.VMEM((2 * depth, width), jnp.bfloat16),
            pltpu.VMEM((depth, width), jnp.bfloat16),
            pltpu.VMEM((depth, width), jnp.float32),
            pltpu.VMEM((depth, rim), jnp.float32),
        ],
        compiler_params=pltpu.CompilerParams(vmem_limit_bytes=40 * 1024 * 1024),
        cost_estimate=pl.CostEstimate(
            flops=12 * depth * depth * width, bytes_accessed=8 << 20, transcendentals=depth * width
        ),
    )(*lists, agg, own, before, after, values, w_in, w_out, cot)


def after_kernel(*refs):
    lists, (both_ref, values_ref, middle_ref) = refs[:4], refs[4:]
    depth = middle_ref.shape[0]
    middle_ref[...] = both_ref[:depth].astype(jnp.float32)
    add_slots(lists, OWN, both_ref.at[pl.ds(depth, depth)], middle_ref, values_ref, False)


def after_step(lists, both, values):
    return pl.pallas_call(
        after_kernel,
        out_shape=jax.ShapeDtypeStruct((both.shape[0] // 2, both.shape[1]), jnp.float32),
        in_specs=[SMEM] * 4 + [VMEM] * 2,
        out_specs=VMEM,
        compiler_params=pltpu.CompilerParams(vmem_limit_bytes=24 * 1024 * 1024),
        cost_estimate=pl.CostEstimate(flops=1 << 28, bytes_accessed=6 << 20, transcendentals=0),
    )(*lists, both, values)


def total_kernel(middle_ref, prev_ref, next_ref, out_ref):
    width, rim = middle_ref.shape[1], prev_ref.shape[1]
    edges = sorted({0, min(rim, width - rim), max(rim, width - rim), width})
    for at, end in zip(edges, edges[1:]):
        part = middle_ref[:, at:end]
        if at < rim:
            part = part + prev_ref[:, at:end].astype(jnp.float32)
        if at >= width - rim:
            here = at - (width - rim)
            part = part + next_ref[:, here : here + end - at].astype(jnp.float32)
        out_ref[:, at:end] = part.astype(jnp.bfloat16)


def total_step(middle, from_prev, from_next):
    return pl.pallas_call(
        total_kernel,
        out_shape=jax.ShapeDtypeStruct(middle.shape, jnp.bfloat16),
        in_specs=[VMEM] * 3,
        out_specs=VMEM,
        compiler_params=pltpu.CompilerParams(vmem_limit_bytes=24 * 1024 * 1024),
        cost_estimate=pl.CostEstimate(flops=0, bytes_accessed=4 << 20, transcendentals=0),
    )(middle, from_prev, from_next)


def cut_kernel(pos_ref, features_ref, *refs):
    piece_refs, sems = refs[:-1], refs[-1]
    pieces, width = len(piece_refs), piece_refs[0].shape[1]
    copies = []
    for step, piece_ref in enumerate(piece_refs):
        dest = lax.rem(pos_ref[0] + step, pieces)
        part = pl.ds(pl.multiple_of(dest * width, BLK), width)
        copies.append(pltpu.make_async_copy(features_ref.at[:, part], piece_ref, sems.at[step]))
    for copy in copies:
        copy.start()
    for copy in copies:
        copy.wait()


def cut_step(pos, features, pieces):
    height, width = features.shape[0], features.shape[1] // pieces
    return pl.pallas_call(
        cut_kernel,
        out_shape=(jax.ShapeDtypeStruct((height, width), features.dtype),) * pieces,
        in_specs=[SMEM, pl.BlockSpec(memory_space=pl.ANY)],
        out_specs=(VMEM,) * pieces,
        scratch_shapes=[pltpu.SemaphoreType.DMA((pieces,))],
        compiler_params=pltpu.CompilerParams(vmem_limit_bytes=16 * 1024 * 1024),
        cost_estimate=pl.CostEstimate(flops=0, bytes_accessed=2 << 20, transcendentals=0),
    )(pos, features)


def join_kernel(pos_ref, *refs):
    piece_refs, (own_ref, head_ref, tail_ref) = refs[:-3], refs[-3:]
    pieces = len(piece_refs)
    height, width = piece_refs[0].shape
    rim = head_ref.shape[1]
    for step, piece_ref in enumerate(piece_refs):
        source = lax.rem(pos_ref[0] + pieces - step, pieces)
        rows = pl.ds(pl.multiple_of(source * height, height), height)
        own_ref[rows, :] = piece_ref[...]
        head_ref[rows, :] = piece_ref[:, :rim]
        tail_ref[rows, :] = piece_ref[:, width - rim :]


def join_step(pos, received, rim):
    pieces = len(received)
    height, width = received[0].shape
    depth, kind = pieces * height, received[0].dtype
    edge = jax.ShapeDtypeStruct((depth, rim), kind)
    return pl.pallas_call(
        join_kernel,
        out_shape=(jax.ShapeDtypeStruct((depth, width), kind), edge, edge),
        in_specs=[SMEM] + [VMEM] * pieces,
        out_specs=(VMEM,) * 3,
        compiler_params=pltpu.CompilerParams(vmem_limit_bytes=16 * 1024 * 1024),
        cost_estimate=pl.CostEstimate(flops=0, bytes_accessed=4 << 20, transcendentals=0),
    )(pos, *received)


def on_device(
    features, block_row, block_col, block_count, block_values, w_self, w_neigh, cotangent
):
    rows_part = features.shape[1]
    depth, width = cotangent.shape
    rim = REACH * BLK
    chunk = width // BLK
    pos = lax.axis_index("feat").astype(jnp.int32)[None]
    lists = list_step(block_row[0], block_col[0], block_count, pos, chunk)
    w_in = jnp.concatenate([w_self.T, w_neigh.T], axis=1)
    w_out = jnp.concatenate([w_self, w_neigh], axis=0)
    pieces = lax.axis_size("feat")
    received = list(cut_step(pos, features, pieces))
    far = sorted(range(1, pieces), key=lambda step: (abs(2 * step - pieces), step))
    for step in reversed(far):
        received[step] = shifted(received[step], "feat", step)
    own, head, tail = join_step(pos, received, rim)
    before = shifted(tail, RING, 1)
    after = shifted(head, RING, -1)
    agg = before_step(lists, own, block_values)
    left, right, terms, both = local_step(
        lists, agg, own, before, after, block_values, w_in, w_out, cotangent
    )
    plane, line = lax.axis_size(PLANE), lax.axis_size(LINE)
    share = 2 * depth // plane
    from_next = shifted(left, RING, -1)
    from_prev = shifted(right, RING, 1)
    parts = lax.all_to_all(terms, PLANE, split_axis=0, concat_axis=0, tiled=True)
    partial = parts.reshape(plane, share, depth).sum(0).astype(jnp.bfloat16)
    partial, used = lax.optimization_barrier((partial, lists[0]))
    middle = after_step([used, *lists[1:]], both, block_values)
    copies = jnp.broadcast_to(partial[None], (line, share, depth))
    copies = lax.all_to_all(copies, LINE, split_axis=0, concat_axis=0, tiled=True)
    factor = 1.0 / math.sqrt(rows_part * lax.axis_size(DOM))
    grads = copies.reshape(line, share, depth).astype(jnp.float32).sum(0) * factor
    total = total_step(middle, from_prev, from_next)
    total, grads = lax.optimization_barrier((total, grads.astype(jnp.bfloat16)))
    feature_grad = lax.all_to_all(total, "feat", split_axis=0, concat_axis=1, tiled=True)
    grads = collected(grads)
    return (feature_grad, grads[:depth], grads[depth:])


def solution(mesh):
    fine = Mesh(mesh.devices.reshape(2, 4, 4, 2, 8), RING)
    return jax.shard_map(
        on_device,
        mesh=fine,
        in_specs=(
            P("feat", DOM),
            P(DOM, None),
            P(DOM, None),
            P(DOM),
            P(DOM, None, None),
            P(),
            P(),
            P(None, RING),
        ),
        out_specs=(P("feat", DOM), P(), P()),
        check_vma=False,
    )
```
